256 devices in a mesh: section: 16 (over y_hi, z), dp: 16 (over x, y_lo, core).
Axes of the slice: x: 4, y: 4 (y_hi: 2, y_lo: 2; y = y_hi * 2 + y_lo), z: 8, core: 2. Of those that a mesh axis runs over, the one named last changes fastest.
Arguments:
- parked: bfloat16 [16, 4, 512, 8192], P('section', None, 'dp'), may hold values from -40 to 40
- cotangent: bfloat16 [4, 512, 8192], P(None, 'dp'), may hold values from -12 to 12
- park_table: int32 [16, 4], replicated, may hold values from 0 to 3, each once within a row
- run_order: int32 [4], replicated, may hold values from 0 to 3, each once
- norm_gain: float32 [16, 8192], P('section'), may hold values from 0.25 to 1.75
- down_weight: bfloat16 [16, 8192, 128], P('section'), may hold values from -0.06629126 to 0.06629126
- up_weight: bfloat16 [16, 128, 8192], P('section'), may hold values from -0.13258252 to 0.13258252
Outputs:
- input_grads: bfloat16 [16, 4, 512, 8192], P('section', None, 'dp')
- grad_down: float32 [16, 8192, 128], P('section', 'dp')
- grad_up: float32 [16, 128, 8192], P('section', None, 'dp')
The draws below stay inside these ranges and needn't reach their ends.
Inputs may be any that keep to these rules, and one draw needn't show every extreme that they name: Each row of park_table names every micro-batch once. `run_order`: names every micro-batch once.
All inputs are finite; a program needn't handle non-finite values.
Results may differ from the reference program's by a relative error of at most 0.024.
Values may be sent and summed in bfloat16 or wider, within the bound.
No kernel may reach another device: no remote copies, remote signals or barrier semaphores. Data moves between devices by JAX's collectives and lax.ppermute only.
A program may use at most 192 MiB of HBM per device.

```python
import math
import jax
import jax.numpy as jnp
from jax import lax

D = 8192
R = 128
ROWS = 32
MICRO = 4
SECTIONS = 16
DP_ROWS = 512
N_SECTION = 16
N_DP = 16


def draw_parked(key, part):
    own_key = jax.random.fold_in(key, 11)
    shape = (SECTIONS, MICRO, DP_ROWS, D)
    values = jnp.clip(jax.random.normal(own_key, shape, jnp.float32), -6.0, 6.0)
    return values.astype(jnp.bfloat16)


def draw_cotangent(key, part):
    own_key = jax.random.fold_in(key, 12)
    shape = (MICRO, DP_ROWS, D)
    values = jnp.clip(jax.random.normal(own_key, shape, jnp.float32), -6.0, 6.0)
    return values.astype(jnp.bfloat16)


def draw_down_weight(key, part):
    own_key = jax.random.fold_in(key, 13)
    shape = (SECTIONS, D, R)
    values = jnp.clip(jax.random.normal(own_key, shape, jnp.float32), -6.0, 6.0) / math.sqrt(D)
    return values.astype(jnp.bfloat16)


def draw_up_weight(key, part):
    own_key = jax.random.fold_in(key, 14)
    shape = (SECTIONS, R, D)
    values = jnp.clip(jax.random.normal(own_key, shape, jnp.float32), -6.0, 6.0) * (2.0 / math.sqrt(D))
    return values.astype(jnp.bfloat16)


def setup_inputs(seed: int = 0) -> dict:
    key_list = jax.random.split(jax.random.key(seed), 8)
    parked = draw_parked(jax.random.fold_in(key_list[7], 71), 0)
    cotangent = draw_cotangent(jax.random.fold_in(key_list[7], 71), 0)
    park_table = jax.vmap(lambda own: jax.random.permutation(own, MICRO))(jax.random.split(key_list[2], SECTIONS)).reshape((SECTIONS, MICRO)).astype(jnp.int32)
    run_order = jax.random.permutation(key_list[3], MICRO).astype(jnp.int32)
    norm_gain = jnp.clip(1.0 + 0.15 * jax.random.normal(key_list[4], (SECTIONS, D), jnp.float32), 0.25, 1.75)
    down_weight = draw_down_weight(jax.random.fold_in(key_list[7], 71), 0)
    up_weight = draw_up_weight(jax.random.fold_in(key_list[7], 71), 0)
    return {"parked": parked, "cotangent": cotangent, "park_table": park_table, "run_order": run_order, "norm_gain": norm_gain, "down_weight": down_weight, "up_weight": up_weight}


def layer_back(layer_in, upstream, gain_row, down_local, up_local):
    wide_in = layer_in.astype(jnp.float32)
    scale_inv = lax.rsqrt(lax.optimization_barrier(jnp.mean(wide_in * wide_in, axis=-1, keepdims=True)) + 1e-05)
    normed = wide_in * scale_inv
    hidden = (normed * gain_row).astype(jnp.bfloat16)
    pre_act = jnp.dot(hidden, down_local, preferred_element_type=jnp.float32)
    gate_sig = jax.nn.sigmoid(pre_act)
    gated_out = (pre_act * gate_sig).astype(jnp.bfloat16)
    d_gated = jnp.dot(upstream, up_local.T, preferred_element_type=jnp.float32)
    d_act = (d_gated * gate_sig * (1.0 + pre_act * (1.0 - gate_sig))).astype(jnp.bfloat16)
    d_hidden = jnp.dot(d_act, down_local.T, preferred_element_type=jnp.float32) * gain_row
    inner_mean = lax.optimization_barrier(jnp.mean(d_hidden * normed, axis=-1, keepdims=True))
    d_input = (upstream.astype(jnp.float32) + scale_inv * (d_hidden - normed * inner_mean)).astype(jnp.bfloat16)
    return (hidden, gated_out, d_act, d_input)

def reference(parked, cotangent, park_table, run_order, norm_gain, down_weight, up_weight):
    sections = N_SECTION
    pick_micro = (run_order[:, None] == jnp.arange(MICRO, dtype=jnp.int32)[None, :]).astype(jnp.float32)
    incoming = jnp.einsum('km,mrd->krd', pick_micro, cotangent.astype(jnp.float32)).astype(jnp.bfloat16)
    grad_rows = []
    down_grads = []
    up_grads = []
    for section_pos in range(sections - 1, -1, -1):
        holder = sections - 1 - section_pos
        pick_slot = (run_order[:, None] == park_table[holder][None, :]).astype(jnp.float32)
        inputs = jnp.einsum('ks,srd->krd', pick_slot, parked[holder].astype(jnp.float32)).astype(jnp.bfloat16)
        down_sum = jnp.zeros((N_DP, D, R), jnp.float32)
        up_sum = jnp.zeros((N_DP, R, D), jnp.float32)
        outgoing = []
        for position in range(MICRO):
            hidden, gated_out, d_act, d_input = layer_back(inputs[position], incoming[position], norm_gain[section_pos], down_weight[section_pos], up_weight[section_pos])
            hid_parts = hidden.reshape(N_DP, ROWS, D).astype(jnp.float32)
            act_parts = d_act.reshape(N_DP, ROWS, R).astype(jnp.float32)
            gate_parts = gated_out.reshape(N_DP, ROWS, R).astype(jnp.float32)
            up_parts = incoming[position].reshape(N_DP, ROWS, D).astype(jnp.float32)
            down_sum = down_sum + jnp.einsum('prd,prq->pdq', hid_parts, act_parts)
            up_sum = up_sum + jnp.einsum('prq,prd->pqd', gate_parts, up_parts)
            outgoing.append(d_input)
        incoming = jnp.stack(outgoing)
        grad_rows.append(incoming)
        down_round = lax.optimization_barrier(down_sum.astype(jnp.bfloat16))
        up_round = lax.optimization_barrier(up_sum.astype(jnp.bfloat16))
        down_grads.append(lax.optimization_barrier(jnp.sum(down_round.astype(jnp.float32), axis=0)))
        up_grads.append(lax.optimization_barrier(jnp.sum(up_round.astype(jnp.float32), axis=0)))
    input_grads = jnp.stack(grad_rows[::-1])
    grad_down = jnp.stack(down_grads[::-1])
    grad_up = jnp.stack(up_grads[::-1])
    return (input_grads, grad_down, grad_up)
```

```python
import functools
import jax
import jax.numpy as jnp
from jax import lax
from jax.experimental import pallas as pl
from jax.experimental.pallas import tpu as pltpu
from jax.sharding import PartitionSpec as P

N = 16
BLK = 8
ROWS = 128
ROWN = ROWS // N
F = 512
RANK = 128
WIDTH = N * F
PAIRS = [(j, i) for j in range(BLK - 1, 0, -1) for i in range(j)]
PAIR_AT = {pair: n for n, pair in enumerate(PAIRS)}
NP = len(PAIRS)
VMEM = 56 << 20
BF = jnp.bfloat16
F32 = jnp.float32

NT = (((1,), (1,)), ((), ()))
NN = (((1,), (0,)), ((), ()))
TN = (((0,), (0,)), ((), ()))


def dot(a, b, dims):
    return lax.dot_general(a, b, dims, preferred_element_type=F32)


def cols(m, n=1):
    return slice(m * RANK, (m + n) * RANK)


def call(kernel, outs, **kw):
    return pl.pallas_call(
        kernel,
        out_shape=[jax.ShapeDtypeStruct(s, d) for s, d in outs],
        compiler_params=pltpu.CompilerParams(vmem_limit_bytes=VMEM),
        **kw,
    )


def split_kernel(slots, src, dst):
    for n in range(N):
        dst[n, 0] = src[0, :, n * F : (n + 1) * F]


def split_rows(parked, slots):
    micro, rows, width = parked.shape
    return pl.pallas_call(
        split_kernel,
        grid_spec=pltpu.PrefetchScalarGridSpec(
            num_scalar_prefetch=1,
            grid=(micro,),
            in_specs=[pl.BlockSpec((1, rows, width), lambda k, slots: (slots[k], 0, 0))],
            out_specs=pl.BlockSpec((N, 1, rows, F), lambda k, slots: (0, k, 0, 0)),
        ),
        out_shape=jax.ShapeDtypeStruct((N, micro, rows, F), BF),
        compiler_params=pltpu.CompilerParams(vmem_limit_bytes=VMEM),
    )(slots, parked).reshape(N, micro * rows, F)


def join_kernel(src, dst):
    for n in range(N):
        dst[0, :, n * F : (n + 1) * F] = src[n, 0]


def join_rows(pieces, micro):
    rows = ROWS // micro
    return pl.pallas_call(
        join_kernel,
        grid=(micro,),
        in_specs=[pl.BlockSpec((N, 1, rows, F), lambda k: (0, k, 0, 0))],
        out_specs=pl.BlockSpec((1, rows, N * F), lambda k: (k, 0, 0)),
        out_shape=jax.ShapeDtypeStruct((micro, rows, N * F), BF),
        compiler_params=pltpu.CompilerParams(vmem_limit_bytes=VMEM),
    )(pieces.reshape(N, micro, rows, F))


def weight_kernel(jx, ix, big, up, down, part):
    for s in range(N):
        for p in range(N):
            r, h = p // 2, p % 2
            for c in range(2):
                at = (2 * h + c) * RANK
                up[s, 16 * r : 16 * r + 16, at : at + RANK] = big[p, s, 16 * c : 16 * c + 16, :]
            down[s, 32 * p : 32 * p + 32, :] = big[p, s, 32:64, :]
    for d in range(4):
        part[RANK * d : RANK * (d + 1), :] = dot(down[jx[d]].T, up[ix[d]], NT).astype(BF)


def cross_kernel(first, xs, up, down, *refs):
    base = BLK if first else 0
    cot, pay = refs if first else (None, refs[0])
    at = 0

    def ups(n):
        return up[base : base + n].reshape(n * RANK, F)

    if first:
        pay[:, cols(0, BLK)] = dot(cot[...], ups(BLK), NT).astype(BF)
        at = BLK
    for t in range(BLK):
        pay[:, cols(at + t)] = dot(xs[N - 1 - base - t], down[base + t], NN).astype(BF)
    at += BLK
    for j in range(BLK - 1, 0, -1):
        pay[:, cols(at, j)] = dot(xs[N - 1 - base - j], ups(j), NT).astype(BF)
        at += j
    if first:
        lane = lax.broadcasted_iota(jnp.int32, (ROWS, RANK), 1)
        total = jnp.zeros((ROWS, RANK), F32)
        for s in range(N):
            wide = xs[N - 1 - s].astype(F32)
            power = jnp.sum(wide * wide, axis=1, keepdims=True)
            high = power.astype(BF).astype(F32)
            total = jnp.where(lane == s, high, total)
            total = jnp.where(lane == N + s, power - high, total)
        pay[:, cols(at)] = total.astype(BF)


def rank_kernel(first, *refs):
    if first:
        sums, weights, coef, gates = refs
        c_ref, a_ref, p_ref = sums, sums, sums
        a_at, x_at, p_at, base = BLK, 2 * BLK, 2 * BLK + NP, BLK
    else:
        c_ref, a_ref, p_ref, weights, coef, gates = refs
        a_at, x_at, p_at, base = 0, BLK, 0, 0

    def total(ref, m, n=1):
        return jnp.sum(ref[:, cols(m, n)].astype(F32).reshape(N, ROWN, n * RANK), axis=0)

    power = total(p_ref, p_at)
    grads = [total(c_ref, t) for t in range(BLK)]
    lane = lax.broadcasted_iota(jnp.int32, (ROWN, RANK), 1)
    shares = jnp.zeros((ROWN, RANK), F32)
    cross_at = x_at
    for j in range(BLK - 1, -1, -1):
        s = base + j
        mean = (power[:, s : s + 1] + power[:, N + s : N + s + 1]) * (1.0 / WIDTH)
        scale = lax.rsqrt(mean + 1e-05)
        act = total(a_ref, a_at + j) * scale
        sig = jax.nn.sigmoid(act)
        gates[:, cols(j)] = jnp.tile(act * sig, (N, 1)).astype(BF)
        d_act = grads[j] * sig * (1.0 + act * (1.0 - sig))
        inner = jnp.sum(d_act * act, axis=1, keepdims=True) * (1.0 / WIDTH)
        sent = (d_act * scale).astype(BF)
        share = (inner * scale * scale).astype(BF).astype(F32)
        coef[:, cols(j)] = jnp.tile(d_act * scale, (N, 1)).astype(BF)
        shares = jnp.where(lane == j, share, shares)
        if j:
            mats = []
            for i in range(j):
                gap = j - i
                p, d = (i, gap) if gap <= 4 else (j, BLK - gap)
                mats.append(weights[base + p, RANK * (d - 1) : RANK * d, :])
            step = dot(sent, jnp.concatenate(mats, axis=1), NN)
            step = step - share * total(a_ref, cross_at, j)
            cross_at += j
            for i in range(j):
                grads[i] = grads[i] + step[:, cols(i)]
    coef[:, cols(BLK)] = jnp.tile(shares, (N, 1)).astype(BF)


def update_kernel(first, top, coef, xs, down, *refs):
    base = BLK if first else 0
    if first:
        up, out, pay, carry = refs
    else:
        _, out = refs
    grad = top[...].astype(F32)
    shares = coef[:, cols(BLK)].astype(F32)
    for j in range(BLK - 1, -1, -1):
        low = dot(coef[:, cols(j)], down[j], NT)
        grad = grad + low - shares[:, j : j + 1] * xs[BLK - 1 - j].astype(F32)
        out[j] = grad.astype(BF)
    if first:
        carry[...] = grad
        pay[...] = dot(grad.astype(BF), up[...].reshape(BLK * RANK, F), NT).astype(BF)


def parts_kernel(coef, gates, xs, top, grads, parts):
    for j in range(BLK):
        parts[2 * j] = dot(coef[:, cols(j)].T, xs[BLK - 1 - j], NN).astype(BF)
        upstream = top[...] if j == BLK - 1 else grads[j + 1]
        parts[2 * j + 1] = dot(gates[:, cols(j)].T, upstream, NN).astype(BF)


def sum_kernel(parts, out):
    total = parts[0].astype(F32)
    for n in range(1, N):
        total = total + parts[n].astype(F32)
    out[...] = total


def whole(shape):
    return pl.BlockSpec(shape, lambda n: (0,) * len(shape))


def half(shape, at):
    return pl.BlockSpec(shape, lambda n: (at,) + (0,) * (len(shape) - 1))


def swap(block):
    return lax.all_to_all(block, "section", 0, 0, tiled=True)


def body(parked, cotangent, park_table, run_order, norm_gain, down_weight, up_weight):
    me = lax.axis_index("section")
    rep = lax.axis_index("dp")
    micro, rows, width = cotangent.shape

    gain = norm_gain[0].reshape(N, N, 32, 1)
    down = down_weight[0].reshape(N, N, 32, RANK)
    down = lax.dynamic_index_in_dim(down, rep, 1, keepdims=False).astype(F32)
    down = (down * lax.dynamic_index_in_dim(gain, rep, 1, keepdims=False)).astype(BF)
    up = lax.dynamic_slice_in_dim(up_weight[0], 16 * (rep // 2), 16, 0)
    up = lax.dynamic_index_in_dim(up.reshape(16, N, 2, 2, RANK), rep % 2, 2, keepdims=False)
    up = up.transpose(1, 2, 0, 3).reshape(N, 32, RANK)
    thin = lax.all_to_all(jnp.concatenate([up, down], axis=1), "section", 0, 0)
    big = lax.all_gather(thin, "dp")

    slot_row = lax.dynamic_index_in_dim(park_table, me, 0, keepdims=False)
    hit = (run_order[:, None] == slot_row[None, :]).astype(jnp.int32)
    slots = jnp.sum(hit * jnp.arange(micro, dtype=jnp.int32)[None, :], axis=1)
    xs = lax.all_to_all(split_rows(parked[0], slots), "section", 0, 0)
    cot = lax.dynamic_slice_in_dim(cotangent, me * F, F, 2)
    cot = jnp.take(cot, run_order, axis=0).reshape(ROWS, F)

    side = BLK * (rep // BLK)
    near = rep % BLK
    far = (near + jnp.arange(1, 5, dtype=jnp.int32)) % BLK
    smem = pl.BlockSpec(memory_space=pltpu.SMEM)
    vmem = pl.BlockSpec(memory_space=pltpu.VMEM)
    ups, downs, w_part = call(
        weight_kernel,
        [((N, RANK, F), BF), ((N, F, RANK), BF), ((4 * RANK, RANK), BF)],
        in_specs=[smem, smem, vmem],
    )(side + jnp.maximum(near, far), side + jnp.minimum(near, far), big)
    w_sum = swap(w_part).astype(F32).reshape(N, 4 * RANK // N, RANK).sum(0).astype(BF)
    w_all = swap(jnp.broadcast_to(w_sum[None], (N,) + w_sum.shape).reshape(4 * RANK, RANK))
    w_all = lax.all_gather(w_all, "dp")

    (pay1,) = call(
        functools.partial(cross_kernel, True), [((ROWS, (2 * BLK + NP + 1) * RANK), BF)]
    )(xs, ups, downs, cot)
    got1 = swap(pay1)
    (pay2,) = call(functools.partial(cross_kernel, False), [((ROWS, (BLK + NP) * RANK), BF)])(
        xs, ups, downs
    )
    got2 = swap(pay2)

    rank_outs = [((ROWS, (BLK + 1) * RANK), BF), ((ROWS, BLK * RANK), BF)]
    coef1, gates1 = call(functools.partial(rank_kernel, True), rank_outs)(got1, w_all)
    coef1 = swap(coef1)
    gates1 = swap(gates1)

    half_rows, half_down, half_up = (BLK, ROWS, F), (BLK, F, RANK), (BLK, RANK, F)
    grads1, pay3, carry = call(
        functools.partial(update_kernel, True),
        [((N, ROWS, F), BF), ((ROWS, BLK * RANK), BF), ((ROWS, F), F32)],
        grid=(1,),
        in_specs=[
            whole((ROWS, F)),
            whole(coef1.shape),
            half(half_rows, 0),
            half(half_down, 1),
            half(half_up, 0),
        ],
        out_specs=[half(half_rows, 1), whole((ROWS, BLK * RANK)), whole((ROWS, F))],
    )(cot, coef1, xs, downs, ups)
    got3 = swap(pay3)

    def weight_parts(coef, gates, xs_at, top, top_spec, grads, grads_at):
        (parts,) = call(
            parts_kernel,
            [((N, RANK, F), BF)],
            grid=(1,),
            in_specs=[
                whole(coef.shape),
                whole(gates.shape),
                half(half_rows, xs_at),
                top_spec,
                half(half_rows, grads_at),
            ],
            out_specs=[whole((N, RANK, F))],
        )(coef, gates, xs, top, grads)
        parts = lax.all_to_all(parts, "dp", 0, 0)
        (total,) = call(sum_kernel, [((RANK, F), F32)])(parts)
        return total

    total1 = weight_parts(coef1, gates1, 0, cot, whole((ROWS, F)), grads1, 1)

    power_spec = pl.BlockSpec((ROWS, RANK), lambda n: (0, 2 * BLK + NP))
    coef2, gates2 = call(
        functools.partial(rank_kernel, False),
        rank_outs,
        grid=(1,),
        in_specs=[whole(got3.shape), whole(got2.shape), power_spec, whole(w_all.shape)],
        out_specs=[whole(s) for s, _ in rank_outs],
    )(got3, got2, got1, w_all)
    coef2 = swap(coef2)
    gates2 = swap(gates2)
    (grads2,) = call(
        functools.partial(update_kernel, False),
        [((N, ROWS, F), BF)],
        grid=(1,),
        in_specs=[
            whole((ROWS, F)),
            whole(coef2.shape),
            half(half_rows, 1),
            half(half_down, 0),
            pl.BlockSpec(memory_space=pl.ANY),
        ],
        out_specs=[half(half_rows, 0)],
        input_output_aliases={4: 0},
    )(carry, coef2, xs, downs, grads1)
    out = join_rows(lax.all_to_all(grads2, "section", 0, 0), micro)

    top2 = pl.BlockSpec((None, ROWS, F), lambda n: (BLK, 0, 0))
    total2 = weight_parts(coef2, gates2, 1, grads2, top2, grads2, 0)

    def homeward(total, block, kind):
        route = [
            (f * N + 2 * t + kind, (BLK * block + t) * N + f) for f in range(N) for t in range(BLK)
        ]
        return lax.ppermute(total, ("section", "dp"), route)

    down_grad = homeward(total1, 1, 0) + homeward(total2, 0, 0)
    up_grad = homeward(total1, 1, 1) + homeward(total2, 0, 1)
    own_gain = lax.dynamic_slice_in_dim(norm_gain[0], rep * F, F, 0)
    return (out[None], (down_grad.T * own_gain[:, None])[None], up_grad[None])


def solution(mesh):
    placed = (
        P("section", None, "dp", None),
        P(None, "dp", None),
        P(),
        P(),
        P("section", None),
        P("section", None, None),
        P("section", None, None),
    )
    return jax.shard_map(
        body,
        mesh=mesh,
        in_specs=placed,
        out_specs=(
            P("section", None, "dp", None),
            P("section", "dp", None),
            P("section", None, "dp"),
        ),
        check_vma=False,
    )
```

```python
import functools
import jax
import jax.numpy as jnp
from jax import lax
from jax.experimental import pallas as pl
from jax.experimental.pallas import tpu as pltpu
from jax.sharding import PartitionSpec as P

N = 16
BLK = 8
ROWS = 128
ROWN = ROWS // N
F = 512
RANK = 128
WIDTH = N * F
PAIRS = [(j, i) for j in range(BLK - 1, 0, -1) for i in range(j)]
PAIR_AT = {pair: n for n, pair in enumerate(PAIRS)}
NP = len(PAIRS)
VMEM = 56 << 20
X1, A1 = BLK, BLK + NP
SQ = A1 + BLK
A2 = SQ + 1
X2 = A2 + BLK
MATS = X2 + NP
BF = jnp.bfloat16
F32 = jnp.float32

NT = (((1,), (1,)), ((), ()))
NN = (((1,), (0,)), ((), ()))
TN = (((0,), (0,)), ((), ()))


def dot(a, b, dims):
    return lax.dot_general(a, b, dims, preferred_element_type=F32)


def cols(m, n=1):
    return slice(m * RANK, (m + n) * RANK)


def call(kernel, outs, **kw):
    return pl.pallas_call(
        kernel,
        out_shape=[jax.ShapeDtypeStruct(s, d) for s, d in outs],
        compiler_params=pltpu.CompilerParams(vmem_limit_bytes=VMEM),
        **kw,
    )


def split_kernel(slots, src, dst):
    for n in range(N):
        dst[n, 0] = src[0, :, n * F : (n + 1) * F]


def split_rows(parked, slots):
    micro, rows, width = parked.shape
    return pl.pallas_call(
        split_kernel,
        grid_spec=pltpu.PrefetchScalarGridSpec(
            num_scalar_prefetch=1,
            grid=(micro,),
            in_specs=[pl.BlockSpec((1, rows, width), lambda k, slots: (slots[k], 0, 0))],
            out_specs=pl.BlockSpec((N, 1, rows, F), lambda k, slots: (0, k, 0, 0)),
        ),
        out_shape=jax.ShapeDtypeStruct((N, micro, rows, F), BF),
        compiler_params=pltpu.CompilerParams(vmem_limit_bytes=VMEM),
    )(slots, parked).reshape(N, micro * rows, F)


def join_kernel(src, dst):
    for n in range(N):
        dst[0, :, n * F : (n + 1) * F] = src[n, 0]


def join_rows(pieces, micro):
    rows = ROWS // micro
    return pl.pallas_call(
        join_kernel,
        grid=(micro,),
        in_specs=[pl.BlockSpec((N, 1, rows, F), lambda k: (0, k, 0, 0))],
        out_specs=pl.BlockSpec((1, rows, N * F), lambda k: (k, 0, 0)),
        out_shape=jax.ShapeDtypeStruct((micro, rows, N * F), BF),
        compiler_params=pltpu.CompilerParams(vmem_limit_bytes=VMEM),
    )(pieces.reshape(N, micro, rows, F))


def weight_kernel(big, up, down):
    for s in range(N):
        for p in range(N):
            r, h = p // 2, p % 2
            for c in range(2):
                at = (2 * h + c) * RANK
                up[s, 16 * r : 16 * r + 16, at : at + RANK] = big[p, s, 16 * c : 16 * c + 16, :]
            down[s, 32 * p : 32 * p + 32, :] = big[p, s, 32:64, :]


def pick_kernel(first, down, gain, out):
    row = lax.broadcasted_iota(jnp.int32, (16, RANK), 0)
    lane = lax.broadcasted_iota(jnp.int32, (16, RANK), 1)
    hit = (lane == row + first[0]).astype(F32).astype(BF)
    out[...] = (dot(hit, down[...], NT) * gain[...]).astype(BF)


def product_kernel(wrapped, rows0, rows1, up, down, gain, out):
    for k, rows in enumerate((rows0, rows1)):
        straight = dot(rows[...], up[...], NT)
        scaled = (rows[...].astype(F32) * gain[...]).astype(BF)
        turned = dot(scaled, down[...], NN)
        flag = jnp.full((16, RANK), wrapped[k], jnp.int32)
        out[16 * k : 16 * k + 16, :] = jnp.where(flag > 0, turned, straight).astype(BF)


def cross_kernel(xs, up, down, cot, pay):
    def ups(base, n):
        return up[base : base + n].reshape(n * RANK, F)

    pay[:, cols(0, BLK)] = dot(cot[...], ups(BLK, BLK), NT).astype(BF)
    lane = lax.broadcasted_iota(jnp.int32, (ROWS, RANK), 1)
    total = jnp.zeros((ROWS, RANK), F32)
    for s in range(N):
        own = xs[N - 1 - s]
        base, t = BLK * (s // BLK), s % BLK
        pay[:, cols((A1 if base else A2) + t)] = dot(own, down[s], NN).astype(BF)
        if t:
            at = (X1 if base else X2) + PAIR_AT[t, 0]
            pay[:, cols(at, t)] = dot(own, ups(base, t), NT).astype(BF)
        wide = own.astype(F32)
        power = jnp.sum(wide * wide, axis=1, keepdims=True)
        high = power.astype(BF).astype(F32)
        total = jnp.where(lane == s, high, total)
        total = jnp.where(lane == N + s, power - high, total)
    pay[:, cols(SQ)] = total.astype(BF)


def rank_kernel(first, *refs):
    if first:
        sums, weights, coef, gates = refs
        tops, x_at, base = sums, X1, BLK
    else:
        tops, sums, weights, coef = refs
        x_at, base = X2, 0

    def total(ref, m, n=1):
        return jnp.sum(ref[:, cols(m, n)].astype(F32).reshape(N, ROWN, n * RANK), axis=0)

    power = total(sums, SQ)

    def activation(s):
        mean = (power[:, s : s + 1] + power[:, N + s : N + s + 1]) * (1.0 / WIDTH)
        scale = lax.rsqrt(mean + 1e-05)
        act = total(sums, (A1 if s >= BLK else A2) + s % BLK) * scale
        return scale, act, jax.nn.sigmoid(act)

    if first:
        for s in range(N):
            _, act, sig = activation(s)
            gates[:, cols(s)] = (act * sig).astype(BF)
    grads = [total(tops, t) for t in range(BLK)]
    lane = lax.broadcasted_iota(jnp.int32, (ROWN, RANK), 1)
    shares = jnp.zeros((ROWN, RANK), F32)
    for j in range(BLK - 1, -1, -1):
        scale, act, sig = activation(base + j)
        d_act = grads[j] * sig * (1.0 + act * (1.0 - sig))
        inner = jnp.sum(d_act * act, axis=1, keepdims=True) * (1.0 / WIDTH)
        sent = (d_act * scale).astype(BF)
        share = (inner * scale * scale).astype(BF).astype(F32)
        coef[:, cols(j)] = jnp.tile(d_act * scale, (N, 1)).astype(BF)
        shares = jnp.where(lane == j, share, shares)
        if j:
            mats = []
            for i in range(j):
                gap = j - i
                held, d = (i, gap) if gap <= BLK // 2 else (j, BLK - gap)
                k, odd = (d - 1) // 2, (d - 1) % 2
                tiles = [
                    weights[2 * q + odd, base + held, 16 * k : 16 * k + 16, :]
                    for q in range(RANK // 16)
                ]
                mat = jnp.concatenate(tiles, axis=0)
                mats.append(mat if gap <= BLK // 2 else mat.T)
            step = dot(sent, jnp.concatenate(mats, axis=1), NN)
            step = step - share * total(sums, x_at + PAIR_AT[j, 0], j)
            for i in range(j):
                grads[i] = grads[i] + step[:, cols(i)]
    coef[:, cols(BLK)] = jnp.tile(shares, (N, 1)).astype(BF)


def update_kernel(first, top, coef, xs, down, *refs):
    base = BLK if first else 0
    if first:
        up, out, pay, carry = refs
    else:
        _, out = refs
    grad = top[...].astype(F32)
    shares = coef[:, cols(BLK)].astype(F32)
    for j in range(BLK - 1, -1, -1):
        low = dot(coef[:, cols(j)], down[j], NT)
        grad = grad + low - shares[:, j : j + 1] * xs[BLK - 1 - j].astype(F32)
        out[j] = grad.astype(BF)
    if first:
        carry[...] = grad
        pay[...] = dot(grad.astype(BF), up[...].reshape(BLK * RANK, F), NT).astype(BF)


def parts_kernel(coef, gates, xs, top, grads, parts):
    for j in range(BLK):
        parts[2 * j] = dot(coef[:, cols(j)].T, xs[BLK - 1 - j], NN).astype(BF)
        upstream = top[...] if j == BLK - 1 else grads[j + 1]
        parts[2 * j + 1] = dot(gates[:, cols(j)].T, upstream, NN).astype(BF)


def whole(shape):
    return pl.BlockSpec(shape, lambda n: (0,) * len(shape))


def half(shape, at):
    return pl.BlockSpec(shape, lambda n: (at,) + (0,) * (len(shape) - 1))


def swap(block):
    return lax.all_to_all(block, "section", 0, 0, tiled=True)


def body(parked, cotangent, park_table, run_order, norm_gain, down_weight, up_weight):
    me = lax.axis_index("section")
    rep = lax.axis_index("dp")
    micro, rows, width = cotangent.shape

    gain = lax.dynamic_index_in_dim(norm_gain[0].reshape(N, N, 32), rep, 1, keepdims=False)
    down = down_weight[0].reshape(N, N, 32, RANK)
    down = lax.dynamic_index_in_dim(down, rep, 1, keepdims=False).astype(F32)
    down = (down * gain[:, :, None]).astype(BF)
    up = lax.dynamic_slice_in_dim(up_weight[0], 16 * (rep // 2), 16, 0)
    own_up = up
    up = lax.dynamic_index_in_dim(up.reshape(16, N, 2, 2, RANK), rep % 2, 2, keepdims=False)
    up = up.transpose(1, 2, 0, 3).reshape(N, 32, RANK)
    thin = lax.all_to_all(jnp.concatenate([up, down], axis=1), "section", 0, 0)
    big = lax.all_gather(thin, "dp")

    slot_row = lax.dynamic_index_in_dim(park_table, me, 0, keepdims=False)
    hit = (run_order[:, None] == slot_row[None, :]).astype(jnp.int32)
    slots = jnp.sum(hit * jnp.arange(micro, dtype=jnp.int32)[None, :], axis=1)
    pieces = split_rows(parked[0], slots)
    pieces, _ = lax.optimization_barrier((pieces, thin))
    xs = lax.all_to_all(pieces, "section", 0, 0)
    cot = lax.dynamic_slice_in_dim(cotangent, me * F, F, 2)
    cot = jnp.take(cot, run_order, axis=0).reshape(ROWS, F)

    smem = pl.BlockSpec(memory_space=pltpu.SMEM)
    vmem = pl.BlockSpec(memory_space=pltpu.VMEM)
    local, odd = me % BLK, rep % 2
    (own_down,) = call(pick_kernel, [((16, WIDTH), BF)], in_specs=[smem, vmem, vmem])(
        (16 * (rep // 2)).reshape(1), down_weight[0], norm_gain
    )
    fetched, wraps = [], []
    for k in range(2):
        gap = 2 * k + 1 + odd
        rows_out = jnp.where(local >= gap, own_down, own_up)
        route = []
        for s in range(N):
            for p in range(N):
                low = BLK * (s // BLK) + (s - 2 * k - 1 - p % 2) % BLK
                route.append((s * N + p, low * N + p))
        fetched.append(lax.ppermute(rows_out, ("section", "dp"), route))
        wraps.append((local + gap >= BLK).astype(jnp.int32))
    (w_own,) = call(product_kernel, [((32, RANK), BF)], in_specs=[smem] + [vmem] * 5)(
        jnp.stack(wraps), fetched[0], fetched[1], up_weight[0], down_weight[0], norm_gain
    )
    w_all = lax.all_gather(lax.all_gather(w_own, "section"), "dp")

    ups, downs = call(weight_kernel, [((N, RANK, F), BF), ((N, F, RANK), BF)])(big)
    (pay1,) = call(cross_kernel, [((ROWS, MATS * RANK), BF)])(xs, ups, downs, cot)
    got1 = swap(pay1)
    coef_out = ((ROWS, (BLK + 1) * RANK), BF)
    coef1, gates = call(
        functools.partial(rank_kernel, True), [coef_out, ((ROWN, N * RANK), BF)]
    )(got1, w_all)
    coef1 = swap(coef1)
    gates = lax.all_gather(gates, "section", tiled=True)

    half_rows, half_down, half_up = (BLK, ROWS, F), (BLK, F, RANK), (BLK, RANK, F)
    grads1, pay3, carry = call(
        functools.partial(update_kernel, True),
        [((N, ROWS, F), BF), ((ROWS, BLK * RANK), BF), ((ROWS, F), F32)],
        grid=(1,),
        in_specs=[
            whole((ROWS, F)),
            whole(coef1.shape),
            half(half_rows, 0),
            half(half_down, 1),
            half(half_up, 0),
        ],
        out_specs=[half(half_rows, 1), whole((ROWS, BLK * RANK)), whole((ROWS, F))],
    )(cot, coef1, xs, downs, ups)
    got3 = swap(pay3)

    def weight_parts(coef, block, top, top_spec, grads):
        (parts,) = call(
            parts_kernel,
            [((N, RANK, F), BF)],
            grid=(1,),
            in_specs=[
                whole(coef.shape),
                pl.BlockSpec((ROWS, BLK * RANK), lambda n: (0, block)),
                half(half_rows, 1 - block),
                top_spec,
                half(half_rows, block),
            ],
            out_specs=[whole((N, RANK, F))],
        )(coef, gates, xs, top, grads)
        total = lax.psum_scatter(parts, "dp", scatter_dimension=0, tiled=True)[0]
        home = []
        for kind in range(2):
            route = [
                (f * N + 2 * t + kind, (BLK * block + t) * N + f)
                for f in range(N)
                for t in range(BLK)
            ]
            home.append(lax.ppermute(total, ("section", "dp"), route).astype(F32))
        return home

    home1 = weight_parts(coef1, 1, cot, whole((ROWS, F)), grads1)

    (coef2,) = call(functools.partial(rank_kernel, False), [coef_out])(got3, got1, w_all)
    coef2 = swap(coef2)
    (grads2,) = call(
        functools.partial(update_kernel, False),
        [((N, ROWS, F), BF)],
        grid=(1,),
        in_specs=[
            whole((ROWS, F)),
            whole(coef2.shape),
            half(half_rows, 1),
            half(half_down, 0),
            pl.BlockSpec(memory_space=pl.ANY),
        ],
        out_specs=[half(half_rows, 0)],
        input_output_aliases={4: 0},
    )(carry, coef2, xs, downs, grads1)
    out = join_rows(lax.all_to_all(grads2, "section", 0, 0), micro)

    top2 = pl.BlockSpec((None, ROWS, F), lambda n: (BLK, 0, 0))
    home2 = weight_parts(coef2, 0, grads2, top2, grads2)

    down_grad, up_grad = home1[0] + home2[0], home1[1] + home2[1]
    own_gain = lax.dynamic_slice_in_dim(norm_gain[0], rep * F, F, 0)
    return (out[None], (down_grad.T * own_gain[:, None])[None], up_grad[None])


def solution(mesh):
    placed = (
        P("section", None, "dp", None),
        P(None, "dp", None),
        P(),
        P(),
        P("section", None),
        P("section", None, None),
        P("section", None, None),
    )
    return jax.shard_map(
        body,
        mesh=mesh,
        in_specs=placed,
        out_specs=(
            P("section", None, "dp", None),
            P("section", "dp", None),
            P("section", None, "dp"),
        ),
        check_vma=False,
    )
```

```python
import functools
import jax
import jax.numpy as jnp
from jax import lax
from jax.experimental import pallas as pl
from jax.experimental.pallas import tpu as pltpu
from jax.sharding import PartitionSpec as P

N = 16
BLK = 8
ROWS = 128
ROWN = ROWS // N
F = 512
RANK = 128
WIDTH = N * F
PAIRS = [(j, i) for j in range(BLK - 1, 0, -1) for i in range(j)]
PAIR_AT = {pair: n for n, pair in enumerate(PAIRS)}
NP = len(PAIRS)
VMEM = 56 << 20
SIDE = NP + BLK
X1, A1 = 0, NP
X2, A2 = SIDE, SIDE + NP
SQ = 2 * SIDE
MATS = SQ + 1
BF = jnp.bfloat16
F32 = jnp.float32

HALF = BLK // 2

NT = (((1,), (1,)), ((), ()))
NN = (((1,), (0,)), ((), ()))
TN = (((0,), (0,)), ((), ()))


def dot(a, b, dims):
    return lax.dot_general(a, b, dims, preferred_element_type=F32)


def cols(m, n=1):
    return slice(m * RANK, (m + n) * RANK)


def cost(us):
    return pl.CostEstimate(flops=0, bytes_accessed=int(us * 3e6), transcendentals=0)


def call(kernel, outs, us=4, **kw):
    return pl.pallas_call(
        kernel,
        out_shape=[jax.ShapeDtypeStruct(s, d) for s, d in outs],
        compiler_params=pltpu.CompilerParams(vmem_limit_bytes=VMEM),
        cost_estimate=cost(us),
        **kw,
    )


def turned(tiles):
    quarter = lax.broadcasted_iota(jnp.int32, tiles[0].shape, 1) // 32
    for bit in range(2):
        step = 1 << bit
        low = (quarter >> bit) % 2 == 0
        tiles = [
            jnp.where(low, tiles[b], pltpu.roll(tiles[b + step], 32 * step, 1))
            if (b >> bit) % 2 == 0
            else jnp.where(low, pltpu.roll(tiles[b - step], RANK - 32 * step, 1), tiles[b])
            for b in range(4)
        ]
    return tiles


def split_kernel(slots, src, dst):
    for c in range(4):
        for a in range(4):
            tiles = [
                src[0, :, F * (4 * a + b) + RANK * c : F * (4 * a + b) + RANK * (c + 1)]
                for b in range(4)
            ]
            for m, tile in enumerate(turned([tile.astype(F32) for tile in tiles])):
                dst[4 * c + m, 0, :, cols(a)] = tile.astype(BF)


def split_rows(parked, slots):
    micro, rows, width = parked.shape
    return pl.pallas_call(
        split_kernel,
        grid_spec=pltpu.PrefetchScalarGridSpec(
            num_scalar_prefetch=1,
            grid=(micro,),
            in_specs=[pl.BlockSpec((1, rows, width), lambda k, slots: (slots[k], 0, 0))],
            out_specs=pl.BlockSpec((N, 1, rows, F), lambda k, slots: (0, k, 0, 0)),
        ),
        out_shape=jax.ShapeDtypeStruct((N, micro, rows, F), BF),
        compiler_params=pltpu.CompilerParams(vmem_limit_bytes=VMEM),
        cost_estimate=cost(4),
    )(slots, parked).reshape(N, micro * rows, F)


def join_kernel(src, dst):
    for c in range(4):
        for a in range(4):
            tiles = turned([src[4 * c + m, 0, :, cols(a)].astype(F32) for m in range(4)])
            for b, tile in enumerate(tiles):
                at = F * (4 * a + b) + RANK * c
                dst[0, :, at : at + RANK] = tile.astype(BF)


def join_rows(pieces, micro):
    rows = ROWS // micro
    return pl.pallas_call(
        join_kernel,
        grid=(micro,),
        in_specs=[pl.BlockSpec((N, 1, rows, F), lambda k: (0, k, 0, 0))],
        out_specs=pl.BlockSpec((1, rows, N * F), lambda k: (k, 0, 0)),
        out_shape=jax.ShapeDtypeStruct((micro, rows, N * F), BF),
        compiler_params=pltpu.CompilerParams(vmem_limit_bytes=VMEM),
        cost_estimate=cost(4),
    )(pieces.reshape(N, micro, rows, F))


def thin_kernel(rep, down, up, gain, out):
    row = lax.broadcasted_iota(jnp.int32, (32, F), 0)
    lane = lax.broadcasted_iota(jnp.int32, (32, F), 1)
    for c in range(4):
        for a in range(2):
            at = [F * (4 * a + b) + RANK * c for b in range(4)]
            tiles = turned([up[:, n : n + RANK].astype(F32) for n in at])
            for m, tile in enumerate(tiles):
                out[4 * c + m, 16 * a : 16 * a + 16, :] = tile.astype(BF)
    for f in range(N):
        column = jnp.sum(jnp.where(lane == row + 32 * f, gain[...], 0.0), axis=1, keepdims=True)
        out[f, 32:64, :] = (down[0, f].astype(F32) * column).astype(BF)


def thin_weights(rep, down, up, gain):
    return pl.pallas_call(
        thin_kernel,
        grid_spec=pltpu.PrefetchScalarGridSpec(
            num_scalar_prefetch=1,
            grid=(1,),
            in_specs=[
                pl.BlockSpec((1, N, 32, RANK), lambda n, rep: (rep[0], 0, 0, 0)),
                pl.BlockSpec((16, WIDTH // 2), lambda n, rep: (rep[0] // 2, rep[0] % 2)),
                pl.BlockSpec((1, F), lambda n, rep: (0, rep[0])),
            ],
            out_specs=pl.BlockSpec((N, 64, RANK), lambda n, rep: (0, 0, 0)),
        ),
        out_shape=jax.ShapeDtypeStruct((N, 64, RANK), BF),
        compiler_params=pltpu.CompilerParams(vmem_limit_bytes=VMEM),
        cost_estimate=cost(2),
    )(rep.reshape(1), down.reshape(N, N, 32, RANK), up, gain)


def weight_kernel(jx, ix, big, up, down, part):
    for s in range(N):
        for p in range(N):
            r, h = p // 2, p % 2
            for c in range(2):
                at = (2 * h + c) * RANK
                up[s, 16 * r : 16 * r + 16, at : at + RANK] = big[p, s, 16 * c : 16 * c + 16, :]
            down[s, 32 * p : 32 * p + 32, :] = big[p, s, 32:64, :]
    for d in range(HALF):
        part[cols(d), :] = dot(down[jx[d]].T, up[ix[d]], NT).astype(BF)


def top_kernel(order, cot, up, out):
    out[...] = dot(cot[0], up[...], NT).astype(BF)


def top_products(cotangent, order, up):
    micro, rows, width = cotangent.shape
    return pl.pallas_call(
        top_kernel,
        grid_spec=pltpu.PrefetchScalarGridSpec(
            num_scalar_prefetch=1,
            grid=(micro,),
            in_specs=[
                pl.BlockSpec((1, rows, width), lambda k, order: (order[k], 0, 0)),
                pl.BlockSpec((RANK, width), lambda k, order: (0, 0)),
            ],
            out_specs=pl.BlockSpec((rows, RANK), lambda k, order: (k, 0)),
        ),
        out_shape=jax.ShapeDtypeStruct((ROWS, RANK), BF),
        compiler_params=pltpu.CompilerParams(vmem_limit_bytes=VMEM),
        cost_estimate=cost(8),
    )(order, cotangent, up)


def cross_kernel(xs, up, down, pay):
    def ups(base, n):
        return up[base : base + n].reshape(n * RANK, F)

    lane = lax.broadcasted_iota(jnp.int32, (ROWS, RANK), 1)
    total = jnp.zeros((ROWS, RANK), F32)
    for s in range(N):
        own = xs[N - 1 - s]
        base, t = BLK * (s // BLK), s % BLK
        pay[:, cols((A1 if base else A2) + t)] = dot(own, down[s], NN).astype(BF)
        if t:
            at = (X1 if base else X2) + PAIR_AT[t, 0]
            pay[:, cols(at, t)] = dot(own, ups(base, t), NT).astype(BF)
        wide = own.astype(F32)
        power = jnp.sum(wide * wide, axis=1, keepdims=True)
        high = power.astype(BF).astype(F32)
        total = jnp.where(lane == s, high, total)
        total = jnp.where(lane == N + s, power - high, total)
    pay[:, cols(SQ)] = total.astype(BF)


def rank_kernel(first, tops, sums, power, weights, coef):
    base = BLK if first else 0

    def total(ref, m, n=1):
        return jnp.sum(ref[:, cols(m, n)].astype(F32).reshape(N, ROWN, n * RANK), axis=0)

    power = total(power, 0)

    def activation(s):
        mean = (power[:, s : s + 1] + power[:, N + s : N + s + 1]) * (1.0 / WIDTH)
        scale = lax.rsqrt(mean + 1e-05)
        act = total(sums, A1 + s % BLK) * scale
        return scale, act, jax.nn.sigmoid(act)

    if first:
        grads = [tops[ROWN * (BLK + t) : ROWN * (BLK + t + 1), :] for t in range(BLK)]
    else:
        grads = [total(tops, t) for t in range(BLK)]
    lane = lax.broadcasted_iota(jnp.int32, (ROWN, RANK), 1)
    shares = jnp.zeros((ROWN, RANK), F32)
    for j in range(BLK - 1, -1, -1):
        scale, act, sig = activation(base + j)
        d_act = grads[j] * sig * (1.0 + act * (1.0 - sig))
        inner = jnp.sum(d_act * act, axis=1, keepdims=True) * (1.0 / WIDTH)
        sent = (d_act * scale).astype(BF)
        share = (inner * scale * scale).astype(BF).astype(F32)
        coef[:, cols(j)] = jnp.tile(d_act * scale, (N, 1)).astype(BF)
        coef[:, cols(BLK + 1 + j)] = jnp.tile(act * sig, (N, 1)).astype(BF)
        shares = jnp.where(lane == j, share, shares)
        if j:
            mats = []
            for i in range(j):
                gap = j - i
                held, d = (i, gap) if gap <= HALF else (j, BLK - gap)
                mats.append(weights[held, cols(d - 1), :])
            step = dot(sent, jnp.concatenate(mats, axis=1), NN)
            step = step - share * total(sums, X1 + PAIR_AT[j, 0], j)
            for i in range(j):
                grads[i] = grads[i] + step[:, cols(i)]
    coef[:, cols(BLK)] = jnp.tile(shares, (N, 1)).astype(BF)


def update_kernel(first, top, coef, xs, down, *refs):
    base = BLK if first else 0
    if first:
        up, out, pay, carry = refs
    else:
        _, out = refs
    grad = top[...].astype(F32)
    shares = coef[:, cols(BLK)].astype(F32)
    for j in range(BLK - 1, -1, -1):
        low = dot(coef[:, cols(j)], down[j], NT)
        grad = grad + low - shares[:, j : j + 1] * xs[BLK - 1 - j].astype(F32)
        out[j] = grad.astype(BF)
    if first:
        carry[...] = grad
        pay[...] = dot(grad.astype(BF), up[...].reshape(BLK * RANK, F), NT).astype(BF)


def parts_kernel(coef, xs, top, grads, parts):
    for j in range(BLK):
        upstream = top[...] if j == BLK - 1 else grads[j + 1]
        down = dot(xs[BLK - 1 - j], coef[:, cols(j)], TN).astype(BF)
        up = dot(upstream, coef[:, cols(BLK + 1 + j)], TN).astype(BF)
        for p in range(N):
            parts[p, j, 0:32, :] = down[32 * p : 32 * p + 32]
            parts[p, j, 32:64, :] = up[32 * p : 32 * p + 32]


def after(block, *others):
    return lax.optimization_barrier((block, *others))[0]


def whole(shape):
    return pl.BlockSpec(shape, lambda n: (0,) * len(shape))


def half(shape, at):
    return pl.BlockSpec(shape, lambda n: (at,) + (0,) * (len(shape) - 1))


def swap(block):
    return lax.all_to_all(block, "section", 0, 0, tiled=True)


def body(parked, cotangent, park_table, run_order, norm_gain, down_weight, up_weight):
    me = lax.axis_index("section")
    rep = lax.axis_index("dp")
    micro, rows, width = cotangent.shape

    thin = thin_weights(rep, down_weight[0], up_weight[0], norm_gain)
    thin = lax.all_to_all(thin, "section", 0, 0)
    big = lax.all_gather(thin, "dp")

    slot_row = lax.dynamic_index_in_dim(park_table, me, 0, keepdims=False)
    hit = (run_order[:, None] == slot_row[None, :]).astype(jnp.int32)
    slots = jnp.sum(hit * jnp.arange(micro, dtype=jnp.int32)[None, :], axis=1)
    pieces = split_rows(parked[0], slots)
    xs = lax.all_to_all(after(pieces, thin), "section", 0, 0)
    cot = lax.dynamic_index_in_dim(split_rows(cotangent, run_order), me, 0, keepdims=False)

    side, near = BLK * (rep // BLK), rep % BLK
    far = (near + jnp.arange(1, HALF + 1, dtype=jnp.int32)) % BLK
    smem = pl.BlockSpec(memory_space=pltpu.SMEM)
    ups, downs, w_part = call(
        weight_kernel,
        [((N, RANK, F), BF), ((N, F, RANK), BF), ((HALF * RANK, RANK), BF)],
        in_specs=[smem, smem, pl.BlockSpec(memory_space=pltpu.VMEM)],
    )(side + jnp.maximum(near, far), side + jnp.minimum(near, far), big)
    tops = top_products(cotangent, run_order, up_weight[0]).reshape(N, ROWN, RANK)
    mixed = jnp.concatenate([w_part.reshape(N, -1, RANK), tops], axis=1)
    mixed = lax.all_to_all(after(mixed, xs), "section", 0, 0).astype(F32)
    w_sum = mixed[:, :-ROWN].sum(0).astype(BF)
    tops = mixed[:, -ROWN:].reshape(N * ROWN, RANK)
    w_all = swap(jnp.broadcast_to(w_sum[None], (N,) + w_sum.shape).reshape(-1, RANK))

    (pay1,) = call(cross_kernel, [((ROWS, MATS * RANK), BF)])(xs, ups, downs)
    got1 = swap(after(pay1, w_all))
    w_all = lax.all_gather(w_all, "dp").reshape(N, HALF * RANK, RANK)
    coef_out = ((ROWS, (2 * BLK + 1) * RANK), BF)

    def rank_steps(block, tops):
        return call(
            functools.partial(rank_kernel, block == 1),
            [coef_out],
            grid=(1,),
            in_specs=[
                whole(tops.shape),
                pl.BlockSpec((ROWS, SIDE * RANK), lambda n: (0, 1 - block)),
                pl.BlockSpec((ROWS, RANK), lambda n: (0, SQ)),
                half((BLK,) + w_all.shape[1:], block),
            ],
            out_specs=[whole(coef_out[0])],
        )(tops, got1, got1, w_all)[0]

    coef1 = rank_steps(1, tops)
    coef1 = swap(coef1)

    half_rows, half_down, half_up = (BLK, ROWS, F), (BLK, F, RANK), (BLK, RANK, F)
    grads1, pay3, carry = call(
        functools.partial(update_kernel, True),
        [((N, ROWS, F), BF), ((ROWS, BLK * RANK), BF), ((ROWS, F), F32)],
        grid=(1,),
        in_specs=[
            whole((ROWS, F)),
            whole(coef1.shape),
            half(half_rows, 0),
            half(half_down, 1),
            half(half_up, 0),
        ],
        out_specs=[half(half_rows, 1), whole((ROWS, BLK * RANK)), whole((ROWS, F))],
    )(cot, coef1, xs, downs, ups)
    got3 = swap(pay3)

    def weight_parts(coef, block, top, top_spec, grads):
        (parts,) = call(
            parts_kernel,
            [((N, BLK, 64, RANK), BF)],
            grid=(1,),
            in_specs=[
                whole(coef.shape),
                half(half_rows, 1 - block),
                top_spec,
                half(half_rows, block),
            ],
            out_specs=[whole((N, BLK, 64, RANK))],
        )(coef, xs, top, grads)
        return parts

    def reduced(parts):
        return lax.psum_scatter(parts, "dp", scatter_dimension=0, tiled=True)[0]

    parts1 = weight_parts(coef1, 1, cot, whole((ROWS, F)), grads1)
    got3 = after(got3, parts1)
    total1 = reduced(parts1)

    coef2 = rank_steps(0, got3)
    coef2 = swap(coef2)
    (grads2,) = call(
        functools.partial(update_kernel, False),
        [((N, ROWS, F), BF)],
        grid=(1,),
        in_specs=[
            whole((ROWS, F)),
            whole(coef2.shape),
            half(half_rows, 1),
            half(half_down, 0),
            pl.BlockSpec(memory_space=pl.ANY),
        ],
        out_specs=[half(half_rows, 0)],
        input_output_aliases={4: 0},
    )(carry, coef2, xs, downs, grads1)
    top2 = pl.BlockSpec((None, ROWS, F), lambda n: (BLK, 0, 0))
    parts2 = weight_parts(coef2, 0, grads2, top2, grads2)
    out = join_rows(lax.all_to_all(grads2, "section", 0, 0), micro)
    totals = jnp.concatenate([reduced(parts2), total1])
    totals = lax.all_to_all(totals, "section", 0, 0).astype(F32)

    down_grad = totals[:, :32].reshape(F, RANK)
    up_grad = totals[:, 32:].reshape(F, RANK).T
    own_gain = lax.dynamic_slice_in_dim(norm_gain[0], rep * F, F, 0)
    return (out[None], (down_grad * own_gain[:, None])[None], up_grad[None])


def solution(mesh):
    placed = (
        P("section", None, "dp", None),
        P(None, "dp", None),
        P(),
        P(),
        P("section", None),
        P("section", None, None),
        P("section", None, None),
    )
    return jax.shard_map(
        body,
        mesh=mesh,
        in_specs=placed,
        out_specs=(
            P("section", None, "dp", None),
            P("section", "dp", None),
            P("section", None, "dp"),
        ),
        check_vma=False,
    )
```

```python
import functools
import jax
import jax.numpy as jnp
from jax import lax
from jax.experimental import pallas as pl
from jax.experimental.pallas import tpu as pltpu
from jax.sharding import PartitionSpec as P

N = 16
BLK = 8
ROWS = 128
ROWN = ROWS // N
F = 512
RANK = 128
WIDTH = N * F
PAIRS = [(j, i) for j in range(BLK - 1, 0, -1) for i in range(j)]
PAIR_AT = {pair: n for n, pair in enumerate(PAIRS)}
NP = len(PAIRS)
VMEM = 62 << 20
SIDE = NP + BLK
X1, A1 = 0, NP
X2, A2 = SIDE, SIDE + NP
SQ = 2 * SIDE
MATS = SQ + 1
BF = jnp.bfloat16
F32 = jnp.float32

HALF = BLK // 2
SENT = ROWS + 16

NT = (((1,), (1,)), ((), ()))
NN = (((1,), (0,)), ((), ()))
TN = (((0,), (0,)), ((), ()))


def dot(a, b, dims):
    return lax.dot_general(a, b, dims, preferred_element_type=F32)


def cols(m, n=1):
    return slice(m * RANK, (m + n) * RANK)


def cost(us):
    return pl.CostEstimate(flops=0, bytes_accessed=int(us * 3e6), transcendentals=0)


def call(kernel, outs, us=4, **kw):
    return pl.pallas_call(
        kernel,
        out_shape=[jax.ShapeDtypeStruct(s, d) for s, d in outs],
        compiler_params=pltpu.CompilerParams(vmem_limit_bytes=VMEM),
        cost_estimate=cost(us),
        **kw,
    )


def turned(tiles):
    quarter = lax.broadcasted_iota(jnp.int32, tiles[0].shape, 1) // 32
    for bit in range(2):
        step = 1 << bit
        low = (quarter >> bit) % 2 == 0
        tiles = [
            jnp.where(low, tiles[b], pltpu.roll(tiles[b + step], 32 * step, 1))
            if (b >> bit) % 2 == 0
            else jnp.where(low, pltpu.roll(tiles[b - step], RANK - 32 * step, 1), tiles[b])
            for b in range(4)
        ]
    return tiles


def split_kernel(slots, src, dst):
    for c in range(4):
        for a in range(4):
            tiles = [
                src[0, :, F * (4 * a + b) + RANK * c : F * (4 * a + b) + RANK * (c + 1)]
                for b in range(4)
            ]
            for m, tile in enumerate(turned(tiles)):
                dst[4 * c + m, 0, :, cols(a)] = tile


def split_rows(parked, slots):
    micro, rows, width = parked.shape
    return pl.pallas_call(
        split_kernel,
        grid_spec=pltpu.PrefetchScalarGridSpec(
            num_scalar_prefetch=1,
            grid=(micro,),
            in_specs=[pl.BlockSpec((1, rows, width), lambda k, slots: (slots[k], 0, 0))],
            out_specs=pl.BlockSpec((N, 1, rows, F), lambda k, slots: (0, k, 0, 0)),
        ),
        out_shape=jax.ShapeDtypeStruct((N, micro, rows, F), BF),
        compiler_params=pltpu.CompilerParams(vmem_limit_bytes=VMEM),
        cost_estimate=cost(4),
    )(slots, parked).reshape(N, micro * rows, F)


def join_kernel(src, dst):
    for c in range(4):
        for a in range(4):
            tiles = turned([src[4 * c + m, :, cols(a)] for m in range(4)])
            for b, tile in enumerate(tiles):
                at = F * (4 * a + b) + RANK * c
                dst[0, :, at : at + RANK] = tile


def join_rows(pieces, micro):
    rows = ROWS // micro
    return pl.pallas_call(
        join_kernel,
        grid=(micro,),
        in_specs=[pl.BlockSpec((N, rows, F), lambda k: (0, k, 0))],
        out_specs=pl.BlockSpec((1, rows, N * F), lambda k: (k, 0, 0)),
        out_shape=jax.ShapeDtypeStruct((micro, rows, N * F), BF),
        compiler_params=pltpu.CompilerParams(vmem_limit_bytes=VMEM),
        cost_estimate=cost(4),
    )(pieces)


def thin_kernel(rep, down, up, gain, out):
    row = lax.broadcasted_iota(jnp.int32, (32, F), 0)
    lane = lax.broadcasted_iota(jnp.int32, (32, F), 1)
    for c in range(4):
        for a in range(2):
            at = [F * (4 * a + b) + RANK * c for b in range(4)]
            tiles = turned([up[:, n : n + RANK] for n in at])
            for m, tile in enumerate(tiles):
                out[4 * c + m, 16 * a : 16 * a + 16, :] = tile
    for f in range(N):
        column = jnp.sum(jnp.where(lane == row + 32 * f, gain[...], 0.0), axis=1, keepdims=True)
        out[f, 32:64, :] = (down[0, f].astype(F32) * column).astype(BF)


def thin_weights(rep, down, up, gain):
    return pl.pallas_call(
        thin_kernel,
        grid_spec=pltpu.PrefetchScalarGridSpec(
            num_scalar_prefetch=1,
            grid=(1,),
            in_specs=[
                pl.BlockSpec((1, N, 32, RANK), lambda n, rep: (rep[0], 0, 0, 0)),
                pl.BlockSpec((16, WIDTH // 2), lambda n, rep: (rep[0] // 2, rep[0] % 2)),
                pl.BlockSpec((1, F), lambda n, rep: (0, rep[0])),
            ],
            out_specs=pl.BlockSpec((N, 64, RANK), lambda n, rep: (0, 0, 0)),
        ),
        out_shape=jax.ShapeDtypeStruct((N, 64, RANK), BF),
        compiler_params=pltpu.CompilerParams(vmem_limit_bytes=VMEM),
        cost_estimate=cost(2),
    )(rep.reshape(1), down.reshape(N, N, 32, RANK), up, gain)


def weight_kernel(jx, ix, big, up, down, part):
    for s in range(N):
        for p in range(N):
            r, h = p // 2, p % 2
            for c in range(2):
                at = (2 * h + c) * RANK
                up[s, 16 * r : 16 * r + 16, at : at + RANK] = big[p, s, 16 * c : 16 * c + 16, :]
            down[s, 32 * p : 32 * p + 32, :] = big[p, s, 32:64, :]
    for d in range(HALF):
        part[cols(d), :] = dot(down[jx[d]].T, up[ix[d]], NT).astype(BF)


def top_kernel(order, cot, up, out):
    out[...] = dot(cot[0], up[...], NT).astype(BF)


def top_products(cotangent, order, up):
    micro, rows, width = cotangent.shape
    return pl.pallas_call(
        top_kernel,
        grid_spec=pltpu.PrefetchScalarGridSpec(
            num_scalar_prefetch=1,
            grid=(micro,),
            in_specs=[
                pl.BlockSpec((1, rows, width), lambda k, order: (order[k], 0, 0)),
                pl.BlockSpec((RANK, width), lambda k, order: (0, 0)),
            ],
            out_specs=pl.BlockSpec((rows, RANK), lambda k, order: (k, 0)),
        ),
        out_shape=jax.ShapeDtypeStruct((ROWS, RANK), BF),
        compiler_params=pltpu.CompilerParams(vmem_limit_bytes=VMEM),
        cost_estimate=cost(8),
    )(order, cotangent, up)


def cross_kernel(xs, up, down, pay):
    def ups(base, n):
        return up[base : base + n].reshape(n * RANK, F)

    lane = lax.broadcasted_iota(jnp.int32, (ROWS, RANK), 1)
    total = jnp.zeros((ROWS, RANK), F32)
    for s in range(N):
        own = xs[N - 1 - s]
        base, t = BLK * (s // BLK), s % BLK
        pay[:, cols((A1 if base else A2) + t)] = dot(own, down[s], NN).astype(BF)
        if t:
            at = (X1 if base else X2) + PAIR_AT[t, 0]
            pay[:, cols(at, t)] = dot(own, ups(base, t), NT).astype(BF)
        wide = own.astype(F32)
        power = jnp.sum(wide * wide, axis=1, keepdims=True)
        high = power.astype(BF).astype(F32)
        total = jnp.where(lane == s, high, total)
        total = jnp.where(lane == N + s, power - high, total)
    pay[:, cols(SQ)] = total.astype(BF)


def rank_kernel(first, tops, sums, power, weights, coef):
    base = BLK if first else 0

    def total(ref, m, n=1):
        return jnp.sum(ref[:, cols(m, n)].astype(F32).reshape(N, ROWN, n * RANK), axis=0)

    power = total(power, 0)

    def activation(s):
        mean = (power[:, s : s + 1] + power[:, N + s : N + s + 1]) * (1.0 / WIDTH)
        scale = lax.rsqrt(mean + 1e-05)
        act = total(sums, A1 + s % BLK) * scale
        return scale, act, jax.nn.sigmoid(act)

    if first:
        grads = [tops[ROWN * (BLK + t) : ROWN * (BLK + t + 1), :] for t in range(BLK)]
    else:
        grads = [total(tops, t) for t in range(BLK)]
    lane = lax.broadcasted_iota(jnp.int32, (ROWN, RANK), 1)
    shares = jnp.zeros((ROWN, RANK), F32)
    for j in range(BLK - 1, -1, -1):
        scale, act, sig = activation(base + j)
        d_act = grads[j] * sig * (1.0 + act * (1.0 - sig))
        inner = jnp.sum(d_act * act, axis=1, keepdims=True) * (1.0 / WIDTH)
        sent = (d_act * scale).astype(BF)
        share = (inner * scale * scale).astype(BF).astype(F32)
        coef[:, cols(j)] = jnp.tile(d_act * scale, (N, 1)).astype(BF)
        coef[:, cols(BLK + 1 + j)] = jnp.tile(act * sig, (N, 1)).astype(BF)
        shares = jnp.where(lane == j, share, shares)
        if j:
            mats = []
            for i in range(j):
                gap = j - i
                held, d = (i, gap) if gap <= HALF else (j, BLK - gap)
                mats.append(weights[held, cols(d - 1), :])
            step = dot(sent, jnp.concatenate(mats, axis=1), NN)
            step = step - share * total(sums, X1 + PAIR_AT[j, 0], j)
            for i in range(j):
                grads[i] = grads[i] + step[:, cols(i)]
    coef[:, cols(BLK)] = jnp.tile(shares, (N, 1)).astype(BF)


def update_kernel(first, core, top, coef, xs, down, *refs):
    if first:
        up, out, pay, carry, parts = refs
    else:
        _, out, kept, sent = refs
    grad = top[...].astype(F32)
    shares = coef[:, cols(BLK)].astype(F32)
    for j in range(BLK - 1, -1, -1):
        low = dot(coef[:, cols(j)], down[j], NT)
        grad = grad + low - shares[:, j : j + 1] * xs[BLK - 1 - j].astype(F32)
        out[j] = grad.astype(BF)
    if first:
        carry[...] = grad
        pay[...] = dot(grad.astype(BF), up[...].reshape(BLK * RANK, F), NT).astype(BF)
    own = jnp.full((64, RANK), core[0], jnp.int32) == 0
    for j in range(BLK):
        upstream = out[j + 1] if j < BLK - 1 else top[...].astype(BF)
        down_part = dot(xs[BLK - 1 - j], coef[:, cols(j)], TN)
        up_part = dot(upstream, coef[:, cols(BLK + 1 + j)], TN)
        for n in range(N // 2):
            at = 64 * n
            even = jnp.concatenate([down_part[at : at + 32], up_part[at : at + 32]], axis=0)
            odd = jnp.concatenate(
                [down_part[at + 32 : at + 64], up_part[at + 32 : at + 64]], axis=0
            )
            if first:
                parts[2 * n, j] = even.astype(BF)
                parts[2 * n + 1, j] = odd.astype(BF)
            else:
                kept[n, j] = jnp.where(own, even, odd).astype(BF)
                sent[n, j] = jnp.where(own, odd, even).astype(BF)


def pair_kernel(kept, other, out):
    out[...] = (kept[...].astype(F32) + other[...].astype(F32)).astype(BF)


def replica_parts(kept, sent):
    other = lax.ppermute(sent, "dp", [(p, p ^ 1) for p in range(N)])
    (pairs,) = call(pair_kernel, [(kept.shape, BF)], us=2)(kept, other)
    groups = [list(range(n, N, 2)) for n in range(2)]
    return lax.all_to_all(pairs, "dp", 0, 0, axis_index_groups=groups)


def sum_kernel(first, parts, _, out):
    for t in range(BLK):
        total = parts[0, t].astype(F32)
        for n in range(1, N // 2):
            total = total + parts[n, t].astype(F32)
        total = total.astype(BF)
        for n in range(4):
            out[t, :, cols(n)] = total[16 * n : 16 * n + 16]
            out[BLK + t, :, cols(n)] = first[t, 16 * n : 16 * n + 16, :]


def finish_kernel(rep, src, gain, down, up):
    row = lax.broadcasted_iota(jnp.int32, (32, F), 0)
    lane = lax.broadcasted_iota(jnp.int32, (32, F), 1)
    for m in range(4):
        ups = []
        for f in range(4 * m, 4 * m + 4):
            column = jnp.sum(jnp.where(lane == row + 32 * f, gain[...], 0.0), axis=1, keepdims=True)
            tiles = [src[f, :, cols(n)].astype(F32) for n in range(4)]
            down[32 * f : 32 * f + 32, :] = jnp.concatenate(tiles[:2], axis=0) * column
            ups += tiles[2:]
        up[:, cols(m)] = jnp.concatenate(ups, axis=0).T


def finished(received, rep, gain):
    return pl.pallas_call(
        finish_kernel,
        grid_spec=pltpu.PrefetchScalarGridSpec(
            num_scalar_prefetch=1,
            grid=(1,),
            in_specs=[
                pl.BlockSpec((N, 16, F), lambda n, rep: (0, ROWS // 16, 0)),
                pl.BlockSpec((1, F), lambda n, rep: (0, rep[0])),
            ],
            out_specs=[
                pl.BlockSpec((F, RANK), lambda n, rep: (0, 0)),
                pl.BlockSpec((RANK, F), lambda n, rep: (0, 0)),
            ],
        ),
        out_shape=[
            jax.ShapeDtypeStruct((F, RANK), F32),
            jax.ShapeDtypeStruct((RANK, F), F32),
        ],
        compiler_params=pltpu.CompilerParams(vmem_limit_bytes=VMEM),
        cost_estimate=cost(2),
    )(rep.reshape(1), received, gain)


def tie_kernel(*refs):
    pass


def tie(block, *others):
    anywhere = pl.BlockSpec(memory_space=pl.ANY)
    return call(
        tie_kernel,
        [(block.shape, block.dtype)],
        us=1,
        in_specs=[anywhere] * (1 + len(others)),
        out_specs=[anywhere],
        input_output_aliases={0: 0},
    )(block, *others)[0]


def after(block, *others):
    return lax.optimization_barrier((block, *others))[0]


def whole(shape):
    return pl.BlockSpec(shape, lambda n: (0,) * len(shape))


def half(shape, at):
    return pl.BlockSpec(shape, lambda n: (at,) + (0,) * (len(shape) - 1))


def swap(block):
    return lax.all_to_all(block, "section", 0, 0, tiled=True)


def body(parked, cotangent, park_table, run_order, norm_gain, down_weight, up_weight):
    me = lax.axis_index("section")
    rep = lax.axis_index("dp")
    micro, rows, width = cotangent.shape

    thin = thin_weights(rep, down_weight[0], up_weight[0], norm_gain)
    thin = lax.all_to_all(thin, "section", 0, 0)

    slot_row = lax.dynamic_index_in_dim(park_table, me, 0, keepdims=False)
    hit = (run_order[:, None] == slot_row[None, :]).astype(jnp.int32)
    slots = jnp.sum(hit * jnp.arange(micro, dtype=jnp.int32)[None, :], axis=1)
    pieces = split_rows(parked[0], slots)
    big = lax.all_gather(tie(thin, pieces), "dp")
    xs = lax.all_to_all(after(pieces, thin), "section", 0, 0)
    cot = lax.dynamic_index_in_dim(split_rows(cotangent, run_order), me, 0, keepdims=False)

    side, near = BLK * (rep // BLK), rep % BLK
    far = (near + jnp.arange(1, HALF + 1, dtype=jnp.int32)) % BLK
    smem = pl.BlockSpec(memory_space=pltpu.SMEM)
    ups, downs, w_part = call(
        weight_kernel,
        [((N, RANK, F), BF), ((N, F, RANK), BF), ((HALF * RANK, RANK), BF)],
        in_specs=[smem, smem, pl.BlockSpec(memory_space=pltpu.VMEM)],
    )(side + jnp.maximum(near, far), side + jnp.minimum(near, far), big)
    tops = top_products(cotangent, run_order, up_weight[0]).reshape(N, ROWN, RANK)
    mixed = jnp.concatenate([w_part.reshape(N, -1, RANK), tops], axis=1)
    mixed = lax.all_to_all(after(mixed, xs), "section", 0, 0).astype(F32)
    w_sum = mixed[:, :-ROWN].sum(0).astype(BF)
    tops = mixed[:, -ROWN:].reshape(N * ROWN, RANK)
    w_all = swap(jnp.broadcast_to(w_sum[None], (N,) + w_sum.shape).reshape(-1, RANK))

    (pay1,) = call(cross_kernel, [((ROWS, MATS * RANK), BF)])(xs, ups, downs)
    got1 = swap(after(pay1, w_all))
    w_all = lax.all_gather(w_all, "dp").reshape(N, HALF * RANK, RANK)
    coef_out = ((ROWS, (2 * BLK + 1) * RANK), BF)

    def rank_steps(block, tops):
        return call(
            functools.partial(rank_kernel, block == 1),
            [coef_out],
            grid=(1,),
            in_specs=[
                whole(tops.shape),
                pl.BlockSpec((ROWS, SIDE * RANK), lambda n: (0, 1 - block)),
                pl.BlockSpec((ROWS, RANK), lambda n: (0, SQ)),
                half((BLK,) + w_all.shape[1:], block),
            ],
            out_specs=[whole(coef_out[0])],
        )(tops, got1, got1, w_all)[0]

    coef1 = rank_steps(1, tops)
    coef1 = swap(coef1)

    half_rows, half_down, half_up = (BLK, ROWS, F), (BLK, F, RANK), (BLK, RANK, F)
    core = (rep % 2).reshape(1)
    smem = pl.BlockSpec(memory_space=pltpu.SMEM)
    halves = (N // 2, BLK, 64, RANK)
    grads1, pay3, carry, parts1 = call(
        functools.partial(update_kernel, True),
        [
            ((N, SENT, F), BF),
            ((ROWS, BLK * RANK), BF),
            ((ROWS, F), F32),
            ((N, BLK, 64, RANK), BF),
        ],
        grid=(1,),
        in_specs=[
            smem,
            whole((ROWS, F)),
            whole(coef1.shape),
            half(half_rows, 0),
            half(half_down, 1),
            half(half_up, 0),
        ],
        out_specs=[
            half(half_rows, 1),
            whole((ROWS, BLK * RANK)),
            whole((ROWS, F)),
            whole((N, BLK, 64, RANK)),
        ],
    )(core, cot, coef1, xs, downs, ups)
    got3 = swap(pay3)

    def reduced(parts):
        return lax.psum_scatter(parts, "dp", scatter_dimension=0, tiled=True)[0]

    total1 = reduced(parts1)

    coef2 = rank_steps(0, got3)
    coef2 = swap(coef2)
    grads2, kept, sent = call(
        functools.partial(update_kernel, False),
        [((N, SENT, F), BF), (halves, BF), (halves, BF)],
        grid=(1,),
        in_specs=[
            smem,
            whole((ROWS, F)),
            whole(coef2.shape),
            half(half_rows, 1),
            half(half_down, 0),
            pl.BlockSpec(memory_space=pl.ANY),
        ],
        out_specs=[half(half_rows, 0), whole(halves), whole(halves)],
        input_output_aliases={5: 0},
    )(core, carry, coef2, xs, downs, grads1)
    parts2 = replica_parts(kept, sent)
    (sent,) = call(
        sum_kernel,
        [((N, SENT, F), BF)],
        grid=(1,),
        in_specs=[
            whole(total1.shape),
            whole(parts2.shape),
            pl.BlockSpec(memory_space=pl.ANY),
        ],
        out_specs=[pl.BlockSpec((N, 16, F), lambda n: (0, ROWS // 16, 0))],
        input_output_aliases={2: 0},
    )(total1, parts2, grads2)
    received = lax.all_to_all(sent, "section", 0, 0)
    out = join_rows(received, micro)
    down_grad, up_grad = finished(received, rep, norm_gain)
    return (out[None], down_grad[None], up_grad[None])


def solution(mesh):
    placed = (
        P("section", None, "dp", None),
        P(None, "dp", None),
        P(),
        P(),
        P("section", None),
        P("section", None, None),
        P("section", None, None),
    )
    return jax.shard_map(
        body,
        mesh=mesh,
        in_specs=placed,
        out_specs=(
            P("section", None, "dp", None),
            P("section", "dp", None),
            P("section", None, "dp"),
        ),
        check_vma=False,
    )
```

```python
import functools
import jax
import jax.numpy as jnp
from jax import lax
from jax.experimental import pallas as pl
from jax.experimental.pallas import tpu as pltpu
from jax.sharding import PartitionSpec as P

N = 16
BLK = 8
ROWS = 128
ROWN = ROWS // N
F = 512
RANK = 128
WIDTH = N * F
PAIRS = [(j, i) for j in range(BLK - 1, 0, -1) for i in range(j)]
PAIR_AT = {pair: n for n, pair in enumerate(PAIRS)}
NP = len(PAIRS)
VMEM = (64 << 20) - (384 << 10)
SIDE = NP + BLK
X1, A1 = 0, NP
X2, A2 = SIDE, SIDE + NP
SQ = 2 * SIDE
MATS = SQ + 1
BF = jnp.bfloat16
F32 = jnp.float32

HALF = BLK // 2
SENT = ROWS + 16

NT = (((1,), (1,)), ((), ()))
NN = (((1,), (0,)), ((), ()))
TN = (((0,), (0,)), ((), ()))


def dot(a, b, dims):
    return lax.dot_general(a, b, dims, preferred_element_type=F32)


def cols(m, n=1):
    return slice(m * RANK, (m + n) * RANK)


def cost(us):
    return pl.CostEstimate(flops=0, bytes_accessed=int(us * 3e6), transcendentals=0)


def call(kernel, outs, us=4, **kw):
    return pl.pallas_call(
        kernel,
        out_shape=[jax.ShapeDtypeStruct(s, d) for s, d in outs],
        compiler_params=pltpu.CompilerParams(vmem_limit_bytes=VMEM),
        cost_estimate=cost(us),
        **kw,
    )


def turned(tiles):
    quarter = lax.broadcasted_iota(jnp.int32, tiles[0].shape, 1) // 32
    for bit in range(2):
        step = 1 << bit
        low = (quarter >> bit) % 2 == 0
        tiles = [
            jnp.where(low, tiles[b], pltpu.roll(tiles[b + step], 32 * step, 1))
            if (b >> bit) % 2 == 0
            else jnp.where(low, pltpu.roll(tiles[b - step], RANK - 32 * step, 1), tiles[b])
            for b in range(4)
        ]
    return tiles


def split_kernel(slots, src, dst):
    for c in range(4):
        for a in range(4):
            tiles = [
                src[0, :, F * (4 * a + b) + RANK * c : F * (4 * a + b) + RANK * (c + 1)]
                for b in range(4)
            ]
            for m, tile in enumerate(turned(tiles)):
                dst[4 * c + m, 0, :, cols(a)] = tile


def split_rows(parked, slots):
    micro, rows, width = parked.shape
    return pl.pallas_call(
        split_kernel,
        grid_spec=pltpu.PrefetchScalarGridSpec(
            num_scalar_prefetch=1,
            grid=(micro,),
            in_specs=[pl.BlockSpec((1, rows, width), lambda k, slots: (slots[k], 0, 0))],
            out_specs=pl.BlockSpec((N, 1, rows, F), lambda k, slots: (0, k, 0, 0)),
        ),
        out_shape=jax.ShapeDtypeStruct((N, micro, rows, F), BF),
        compiler_params=pltpu.CompilerParams(vmem_limit_bytes=VMEM),
        cost_estimate=cost(4),
    )(slots, parked).reshape(N, micro * rows, F)


def thin_kernel(rep, down, up, gain, out):
    row = lax.broadcasted_iota(jnp.int32, (32, F), 0)
    lane = lax.broadcasted_iota(jnp.int32, (32, F), 1)
    for c in range(4):
        for a in range(2):
            at = [F * (4 * a + b) + RANK * c for b in range(4)]
            tiles = turned([up[:, n : n + RANK] for n in at])
            for m, tile in enumerate(tiles):
                out[4 * c + m, 16 * a : 16 * a + 16, :] = tile
    for f in range(N):
        column = jnp.sum(jnp.where(lane == row + 32 * f, gain[...], 0.0), axis=1, keepdims=True)
        out[f, 32:64, :] = (down[0, f].astype(F32) * column).astype(BF)


def thin_weights(rep, down, up, gain):
    return pl.pallas_call(
        thin_kernel,
        grid_spec=pltpu.PrefetchScalarGridSpec(
            num_scalar_prefetch=1,
            grid=(1,),
            in_specs=[
                pl.BlockSpec((1, N, 32, RANK), lambda n, rep: (rep[0], 0, 0, 0)),
                pl.BlockSpec((16, WIDTH // 2), lambda n, rep: (rep[0] // 2, rep[0] % 2)),
                pl.BlockSpec((1, F), lambda n, rep: (0, rep[0])),
            ],
            out_specs=pl.BlockSpec((N, 64, RANK), lambda n, rep: (0, 0, 0)),
        ),
        out_shape=jax.ShapeDtypeStruct((N, 64, RANK), BF),
        compiler_params=pltpu.CompilerParams(vmem_limit_bytes=VMEM),
        cost_estimate=cost(2),
    )(rep.reshape(1), down.reshape(N, N, 32, RANK), up, gain)


def weight_kernel(big, up, down):
    for s in range(N):
        for p in range(N):
            r, h = p // 2, p % 2
            for c in range(2):
                at = (2 * h + c) * RANK
                up[s, 16 * r : 16 * r + 16, at : at + RANK] = big[p, s, 16 * c : 16 * c + 16, :]
            down[s, 32 * p : 32 * p + 32, :] = big[p, s, 32:64, :]


def product_kernel(jx, ix, big, out):
    for d in range(HALF):
        tiles = [big[p, ix[d], 16 * c : 16 * c + 16, :] for p in range(N) for c in range(2)]
        rows = [jnp.concatenate(tiles[4 * r : 4 * r + 4], axis=1) for r in range(N // 2)]
        up = jnp.concatenate(rows, axis=0)
        down = jnp.concatenate([big[p, jx[d], 32:64, :] for p in range(N)], axis=0)
        out[cols(d), :] = dot(down.T, up, NT).astype(BF)


def top_kernel(order, cot, up, out):
    out[...] = dot(cot[0], up[...], NT).astype(BF)


def top_products(cotangent, order, up):
    micro, rows, width = cotangent.shape
    return pl.pallas_call(
        top_kernel,
        grid_spec=pltpu.PrefetchScalarGridSpec(
            num_scalar_prefetch=1,
            grid=(micro,),
            in_specs=[
                pl.BlockSpec((1, rows, width), lambda k, order: (order[k], 0, 0)),
                pl.BlockSpec((RANK, width), lambda k, order: (0, 0)),
            ],
            out_specs=pl.BlockSpec((rows, RANK), lambda k, order: (k, 0)),
        ),
        out_shape=jax.ShapeDtypeStruct((ROWS, RANK), BF),
        compiler_params=pltpu.CompilerParams(vmem_limit_bytes=VMEM),
        cost_estimate=cost(8),
    )(order, cotangent, up)


def cross_kernel(xs, up, down, pay):
    def ups(base, n):
        return up[base : base + n].reshape(n * RANK, F)

    lane = lax.broadcasted_iota(jnp.int32, (ROWS, RANK), 1)
    total = jnp.zeros((ROWS, RANK), F32)
    for s in range(N):
        own = xs[N - 1 - s]
        base, t = BLK * (s // BLK), s % BLK
        pay[:, cols((A1 if base else A2) + t)] = dot(own, down[s], NN).astype(BF)
        if t:
            at = (X1 if base else X2) + PAIR_AT[t, 0]
            pay[:, cols(at, t)] = dot(own, ups(base, t), NT).astype(BF)
        wide = own.astype(F32)
        power = jnp.sum(wide * wide, axis=1, keepdims=True)
        high = power.astype(BF).astype(F32)
        total = jnp.where(lane == s, high, total)
        total = jnp.where(lane == N + s, power - high, total)
    pay[:, cols(SQ)] = total.astype(BF)


def rank_kernel(first, tops, sums, power, weights, coef):
    base = BLK if first else 0

    def total(ref, m, n=1):
        return jnp.sum(ref[:, cols(m, n)].astype(F32).reshape(N, ROWN, n * RANK), axis=0)

    power = total(power, 0)

    def activation(s):
        mean = (power[:, s : s + 1] + power[:, N + s : N + s + 1]) * (1.0 / WIDTH)
        scale = lax.rsqrt(mean + 1e-05)
        act = total(sums, A1 + s % BLK) * scale
        return scale, act, jax.nn.sigmoid(act)

    if first:
        grads = [tops[ROWN * (BLK + t) : ROWN * (BLK + t + 1), :] for t in range(BLK)]
    else:
        grads = [total(tops, t) for t in range(BLK)]
    lane = lax.broadcasted_iota(jnp.int32, (ROWN, RANK), 1)
    shares = jnp.zeros((ROWN, RANK), F32)
    for j in range(BLK - 1, -1, -1):
        scale, act, sig = activation(base + j)
        d_act = grads[j] * sig * (1.0 + act * (1.0 - sig))
        inner = jnp.sum(d_act * act, axis=1, keepdims=True) * (1.0 / WIDTH)
        sent = (d_act * scale).astype(BF)
        share = (inner * scale * scale).astype(BF).astype(F32)
        coef[:, cols(j)] = jnp.tile(d_act * scale, (N, 1)).astype(BF)
        coef[:, cols(BLK + 1 + j)] = jnp.tile(act * sig, (N, 1)).astype(BF)
        shares = jnp.where(lane == j, share, shares)
        if j:
            mats = []
            for i in range(j):
                gap = j - i
                held, d = (i, gap) if gap <= HALF else (j, BLK - gap)
                mats.append(weights[held, cols(d - 1), :])
            step = dot(sent, jnp.concatenate(mats, axis=1), NN)
            step = step - share * total(sums, X1 + PAIR_AT[j, 0], j)
            for i in range(j):
                grads[i] = grads[i] + step[:, cols(i)]
    coef[:, cols(BLK)] = jnp.tile(shares, (N, 1)).astype(BF)


def update_kernel(first, core, top, coef, xs, down, *refs):
    if first:
        up, out, pay, carry, parts = refs
    else:
        _, out, kept, sent = refs
    grad = top[...].astype(F32)
    shares = coef[:, cols(BLK)].astype(F32)
    for j in range(BLK - 1, -1, -1):
        low = dot(coef[:, cols(j)], down[j], NT)
        grad = grad + low - shares[:, j : j + 1] * xs[BLK - 1 - j].astype(F32)
        out[j] = grad.astype(BF)
    if first:
        carry[...] = grad
        pay[...] = dot(grad.astype(BF), up[...].reshape(BLK * RANK, F), NT).astype(BF)
    own = jnp.full((64, RANK), core[0], jnp.int32) == 0
    for j in range(BLK):
        upstream = out[j + 1] if j < BLK - 1 else top[...].astype(BF)
        down_part = dot(xs[BLK - 1 - j], coef[:, cols(j)], TN)
        up_part = dot(upstream, coef[:, cols(BLK + 1 + j)], TN)
        for n in range(N // 2):
            at = 64 * n
            even = jnp.concatenate([down_part[at : at + 32], up_part[at : at + 32]], axis=0)
            odd = jnp.concatenate(
                [down_part[at + 32 : at + 64], up_part[at + 32 : at + 64]], axis=0
            )
            if first:
                parts[2 * n, j] = even.astype(BF)
                parts[2 * n + 1, j] = odd.astype(BF)
            else:
                kept[n, j] = jnp.where(own, even, odd).astype(BF)
                sent[n, j] = jnp.where(own, odd, even).astype(BF)


def pair_kernel(kept, other, out):
    out[...] = (kept[...].astype(F32) + other[...].astype(F32)).astype(BF)


def replica_parts(kept, sent):
    other = lax.ppermute(sent, "dp", [(p, p ^ 1) for p in range(N)])
    (pairs,) = call(pair_kernel, [(kept.shape, BF)], us=2)(kept, other)
    groups = [list(range(n, N, 2)) for n in range(2)]
    return lax.all_to_all(pairs, "dp", 0, 0, axis_index_groups=groups)


def sum_kernel(first, parts, _, out):
    for t in range(BLK):
        total = parts[0, t].astype(F32)
        for n in range(1, N // 2):
            total = total + parts[n, t].astype(F32)
        total = total.astype(BF)
        for n in range(4):
            out[t, :, cols(n)] = total[16 * n : 16 * n + 16]
            out[BLK + t, :, cols(n)] = first[t, 16 * n : 16 * n + 16, :]


def finish_kernel(rep, src, sums, gain, out, down, up):
    for c in range(4):
        for a in range(4):
            tiles = turned([src[4 * c + m, :, cols(a)] for m in range(4)])
            for b, tile in enumerate(tiles):
                at = F * (4 * a + b) + RANK * c
                out[0, :, at : at + RANK] = tile

    @pl.when(pl.program_id(0) == 0)
    def _():
        row = lax.broadcasted_iota(jnp.int32, (32, F), 0)
        lane = lax.broadcasted_iota(jnp.int32, (32, F), 1)
        for m in range(4):
            ups = []
            for f in range(4 * m, 4 * m + 4):
                hit = jnp.where(lane == row + 32 * f, gain[...], 0.0)
                column = jnp.sum(hit, axis=1, keepdims=True)
                tiles = [sums[f, :, cols(n)].astype(F32) for n in range(4)]
                down[32 * f : 32 * f + 32, :] = jnp.concatenate(tiles[:2], axis=0) * column
                ups += tiles[2:]
            up[:, cols(m)] = jnp.concatenate(ups, axis=0).T


def finished(received, rep, gain, micro):
    rows = ROWS // micro
    return pl.pallas_call(
        finish_kernel,
        grid_spec=pltpu.PrefetchScalarGridSpec(
            num_scalar_prefetch=1,
            grid=(micro,),
            in_specs=[
                pl.BlockSpec((N, rows, F), lambda k, rep: (0, k, 0)),
                pl.BlockSpec((N, 16, F), lambda k, rep: (0, ROWS // 16, 0)),
                pl.BlockSpec((1, F), lambda k, rep: (0, rep[0])),
            ],
            out_specs=[
                pl.BlockSpec((1, rows, WIDTH), lambda k, rep: (k, 0, 0)),
                pl.BlockSpec((F, RANK), lambda k, rep: (0, 0)),
                pl.BlockSpec((RANK, F), lambda k, rep: (0, 0)),
            ],
        ),
        out_shape=[
            jax.ShapeDtypeStruct((micro, rows, WIDTH), BF),
            jax.ShapeDtypeStruct((F, RANK), F32),
            jax.ShapeDtypeStruct((RANK, F), F32),
        ],
        compiler_params=pltpu.CompilerParams(vmem_limit_bytes=VMEM),
        cost_estimate=cost(5),
    )(rep.reshape(1), received, received, gain)


def tie_kernel(*refs):
    pass


def tie(block, *others):
    anywhere = pl.BlockSpec(memory_space=pl.ANY)
    return call(
        tie_kernel,
        [(block.shape, block.dtype)],
        us=1,
        in_specs=[anywhere] * (1 + len(others)),
        out_specs=[anywhere],
        input_output_aliases={0: 0},
    )(block, *others)[0]


def after(block, *others):
    return lax.optimization_barrier((block, *others))[0]


def whole(shape):
    return pl.BlockSpec(shape, lambda n: (0,) * len(shape))


def half(shape, at):
    return pl.BlockSpec(shape, lambda n: (at,) + (0,) * (len(shape) - 1))


def swap(block):
    return lax.all_to_all(block, "section", 0, 0, tiled=True)


def body(parked, cotangent, park_table, run_order, norm_gain, down_weight, up_weight):
    me = lax.axis_index("section")
    rep = lax.axis_index("dp")
    micro, rows, width = cotangent.shape

    thin = thin_weights(rep, down_weight[0], up_weight[0], norm_gain)
    thin = lax.all_to_all(thin, "section", 0, 0)

    slot_row = lax.dynamic_index_in_dim(park_table, me, 0, keepdims=False)
    hit = (run_order[:, None] == slot_row[None, :]).astype(jnp.int32)
    slots = jnp.sum(hit * jnp.arange(micro, dtype=jnp.int32)[None, :], axis=1)
    pieces = split_rows(parked[0], slots)
    big = lax.all_gather(tie(thin, pieces), "dp")
    xs = lax.all_to_all(after(pieces, thin), "section", 0, 0)
    cot = lax.dynamic_index_in_dim(split_rows(cotangent, run_order), me, 0, keepdims=False)

    side, near = BLK * (rep // BLK), rep % BLK
    far = (near + jnp.arange(1, HALF + 1, dtype=jnp.int32)) % BLK
    smem = pl.BlockSpec(memory_space=pltpu.SMEM)
    (w_part,) = call(
        product_kernel,
        [((HALF * RANK, RANK), BF)],
        in_specs=[smem, smem, pl.BlockSpec(memory_space=pltpu.VMEM)],
    )(side + jnp.maximum(near, far), side + jnp.minimum(near, far), big)
    ups, downs = call(weight_kernel, [((N, RANK, F), BF), ((N, F, RANK), BF)])(big)
    tops = top_products(cotangent, run_order, up_weight[0]).reshape(N, ROWN, RANK)
    mixed = jnp.concatenate([w_part.reshape(N, -1, RANK), tops], axis=1)
    mixed = lax.all_to_all(after(mixed, xs), "section", 0, 0).astype(F32)
    w_sum = mixed[:, :-ROWN].sum(0).astype(BF)
    tops = mixed[:, -ROWN:].reshape(N * ROWN, RANK)
    w_all = jnp.broadcast_to(w_sum[None], (N,) + w_sum.shape).reshape(-1, RANK)
    w_all = swap(tie(w_all, ups))

    (pay1,) = call(cross_kernel, [((ROWS, MATS * RANK), BF)])(xs, ups, downs)
    got1 = swap(after(pay1, w_all))
    w_all = lax.all_gather(w_all, "dp").reshape(N, HALF * RANK, RANK)
    coef_out = ((ROWS, (2 * BLK + 1) * RANK), BF)

    def rank_steps(block, tops):
        return call(
            functools.partial(rank_kernel, block == 1),
            [coef_out],
            grid=(1,),
            in_specs=[
                whole(tops.shape),
                pl.BlockSpec((ROWS, SIDE * RANK), lambda n: (0, 1 - block)),
                pl.BlockSpec((ROWS, RANK), lambda n: (0, SQ)),
                half((BLK,) + w_all.shape[1:], block),
            ],
            out_specs=[whole(coef_out[0])],
        )(tops, got1, got1, w_all)[0]

    coef1 = rank_steps(1, tops)
    coef1 = swap(coef1)

    half_rows, half_down, half_up = (BLK, ROWS, F), (BLK, F, RANK), (BLK, RANK, F)
    core = (rep % 2).reshape(1)
    smem = pl.BlockSpec(memory_space=pltpu.SMEM)
    halves = (N // 2, BLK, 64, RANK)
    grads1, pay3, carry, parts1 = call(
        functools.partial(update_kernel, True),
        [
            ((N, SENT, F), BF),
            ((ROWS, BLK * RANK), BF),
            ((ROWS, F), F32),
            ((N, BLK, 64, RANK), BF),
        ],
        grid=(1,),
        in_specs=[
            smem,
            whole((ROWS, F)),
            whole(coef1.shape),
            half(half_rows, 0),
            half(half_down, 1),
            half(half_up, 0),
        ],
        out_specs=[
            half(half_rows, 1),
            whole((ROWS, BLK * RANK)),
            whole((ROWS, F)),
            whole((N, BLK, 64, RANK)),
        ],
    )(core, cot, coef1, xs, downs, ups)
    got3 = swap(pay3)

    def reduced(parts):
        return lax.psum_scatter(parts, "dp", scatter_dimension=0, tiled=True)[0]

    total1 = reduced(parts1)

    coef2 = rank_steps(0, got3)
    coef2 = swap(coef2)
    grads2, kept, sent = call(
        functools.partial(update_kernel, False),
        [((N, SENT, F), BF), (halves, BF), (halves, BF)],
        grid=(1,),
        in_specs=[
            smem,
            whole((ROWS, F)),
            whole(coef2.shape),
            half(half_rows, 1),
            half(half_down, 0),
            pl.BlockSpec(memory_space=pl.ANY),
        ],
        out_specs=[half(half_rows, 0), whole(halves), whole(halves)],
        input_output_aliases={5: 0},
    )(core, carry, coef2, xs, downs, grads1)
    parts2 = replica_parts(kept, sent)
    (sent,) = call(
        sum_kernel,
        [((N, SENT, F), BF)],
        grid=(1,),
        in_specs=[
            whole(total1.shape),
            whole(parts2.shape),
            pl.BlockSpec(memory_space=pl.ANY),
        ],
        out_specs=[pl.BlockSpec((N, 16, F), lambda n: (0, ROWS // 16, 0))],
        input_output_aliases={2: 0},
    )(total1, parts2, grads2)
    received = lax.all_to_all(sent, "section", 0, 0)
    out, down_grad, up_grad = finished(received, rep, norm_gain, micro)
    return (out[None], down_grad[None], up_grad[None])


def solution(mesh):
    placed = (
        P("section", None, "dp", None),
        P(None, "dp", None),
        P(),
        P(),
        P("section", None),
        P("section", None, None),
        P("section", None, None),
    )
    return jax.shard_map(
        body,
        mesh=mesh,
        in_specs=placed,
        out_specs=(
            P("section", None, "dp", None),
            P("section", "dp", None),
            P("section", None, "dp"),
        ),
        check_vma=False,
    )
```

```python
import functools
import jax
import jax.numpy as jnp
from jax import lax
from jax.experimental import pallas as pl
from jax.experimental.pallas import tpu as pltpu
from jax.sharding import PartitionSpec as P

N = 16
BLK = 8
ROWS = 128
ROWN = ROWS // N
F = 512
RANK = 128
WIDTH = N * F
PAIRS = [(j, i) for j in range(BLK - 1, 0, -1) for i in range(j)]
PAIR_AT = {pair: n for n, pair in enumerate(PAIRS)}
NP = len(PAIRS)
VMEM = (64 << 20) - (384 << 10)
SIDE = NP + BLK
X1, A1 = 0, NP
X2, A2 = SIDE, SIDE + NP
SQ = 2 * SIDE
MATS = SQ + 1
BF = jnp.bfloat16
F32 = jnp.float32

HALF = BLK // 2
SENT = ROWS + 16

NT = (((1,), (1,)), ((), ()))
NN = (((1,), (0,)), ((), ()))
TN = (((0,), (0,)), ((), ()))


def dot(a, b, dims):
    return lax.dot_general(a, b, dims, preferred_element_type=F32)


def cols(m, n=1):
    return slice(m * RANK, (m + n) * RANK)


def cost(us):
    return pl.CostEstimate(flops=0, bytes_accessed=int(us * 3e6), transcendentals=0)


def call(kernel, outs, us=4, **kw):
    return pl.pallas_call(
        kernel,
        out_shape=[jax.ShapeDtypeStruct(s, d) for s, d in outs],
        compiler_params=pltpu.CompilerParams(vmem_limit_bytes=VMEM),
        cost_estimate=cost(us),
        **kw,
    )


def turned(tiles):
    quarter = lax.broadcasted_iota(jnp.int32, tiles[0].shape, 1) // 32
    for bit in range(2):
        step = 1 << bit
        low = (quarter >> bit) % 2 == 0
        tiles = [
            jnp.where(low, tiles[b], pltpu.roll(tiles[b + step], 32 * step, 1))
            if (b >> bit) % 2 == 0
            else jnp.where(low, pltpu.roll(tiles[b - step], RANK - 32 * step, 1), tiles[b])
            for b in range(4)
        ]
    return tiles


def split_kernel(slots, src, dst):
    for c in range(4):
        for a in range(4):
            tiles = [
                src[0, :, F * (4 * a + b) + RANK * c : F * (4 * a + b) + RANK * (c + 1)]
                for b in range(4)
            ]
            for m, tile in enumerate(turned(tiles)):
                dst[4 * c + m, 0, :, cols(a)] = tile


def split_rows(parked, slots):
    micro, rows, width = parked.shape
    return pl.pallas_call(
        split_kernel,
        grid_spec=pltpu.PrefetchScalarGridSpec(
            num_scalar_prefetch=1,
            grid=(micro,),
            in_specs=[pl.BlockSpec((1, rows, width), lambda k, slots: (slots[k], 0, 0))],
            out_specs=pl.BlockSpec((N, 1, rows, F), lambda k, slots: (0, k, 0, 0)),
        ),
        out_shape=jax.ShapeDtypeStruct((N, micro, rows, F), BF),
        compiler_params=pltpu.CompilerParams(vmem_limit_bytes=VMEM),
        cost_estimate=cost(4),
    )(slots, parked).reshape(N, micro * rows, F)


def thin_kernel(rep, down, up, gain, out):
    row = lax.broadcasted_iota(jnp.int32, (32, F), 0)
    lane = lax.broadcasted_iota(jnp.int32, (32, F), 1)
    for c in range(4):
        for a in range(2):
            at = [F * (4 * a + b) + RANK * c for b in range(4)]
            tiles = turned([up[:, n : n + RANK] for n in at])
            for m, tile in enumerate(tiles):
                out[4 * c + m, 16 * a : 16 * a + 16, :] = tile
    for f in range(N):
        column = jnp.sum(jnp.where(lane == row + 32 * f, gain[...], 0.0), axis=1, keepdims=True)
        out[f, 32:64, :] = (down[0, f].astype(F32) * column).astype(BF)


def thin_weights(rep, down, up, gain):
    return pl.pallas_call(
        thin_kernel,
        grid_spec=pltpu.PrefetchScalarGridSpec(
            num_scalar_prefetch=1,
            grid=(1,),
            in_specs=[
                pl.BlockSpec((1, N, 32, RANK), lambda n, rep: (rep[0], 0, 0, 0)),
                pl.BlockSpec((16, WIDTH // 2), lambda n, rep: (rep[0] // 2, rep[0] % 2)),
                pl.BlockSpec((1, F), lambda n, rep: (0, rep[0])),
            ],
            out_specs=pl.BlockSpec((N, 64, RANK), lambda n, rep: (0, 0, 0)),
        ),
        out_shape=jax.ShapeDtypeStruct((N, 64, RANK), BF),
        compiler_params=pltpu.CompilerParams(vmem_limit_bytes=VMEM),
        cost_estimate=cost(2),
    )(rep.reshape(1), down.reshape(N, N, 32, RANK), up, gain)


def layout_kernel(big, xs, up, down, squares):
    lane = lax.broadcasted_iota(jnp.int32, (ROWS, RANK), 1)
    total = jnp.zeros((ROWS, RANK), F32)
    for s in range(N):
        wide = xs[N - 1 - s].astype(F32)
        power = jnp.sum(wide * wide, axis=1, keepdims=True)
        high = power.astype(BF).astype(F32)
        total = jnp.where(lane == s, high, total)
        total = jnp.where(lane == N + s, power - high, total)
    squares[...] = total.astype(BF)
    for s in range(N):
        for p in range(N):
            r, h = p // 2, p % 2
            for c in range(2):
                at = (2 * h + c) * RANK
                up[s, 16 * r : 16 * r + 16, at : at + RANK] = big[p, s, 16 * c : 16 * c + 16, :]
            down[s, 32 * p : 32 * p + 32, :] = big[p, s, 32:64, :]


def product_kernel(jx, ix, big, out):
    for d in range(HALF):
        tiles = [big[p, ix[d], 16 * c : 16 * c + 16, :] for p in range(N) for c in range(2)]
        rows = [jnp.concatenate(tiles[4 * r : 4 * r + 4], axis=1) for r in range(N // 2)]
        up = jnp.concatenate(rows, axis=0)
        down = jnp.concatenate([big[p, jx[d], 32:64, :] for p in range(N)], axis=0)
        out[cols(d), :] = dot(down.T, up, NT).astype(BF)


def top_kernel(order, cot, up, out):
    out[...] = dot(cot[0], up[...], NT).astype(BF)


def top_products(cotangent, order, up):
    micro, rows, width = cotangent.shape
    return pl.pallas_call(
        top_kernel,
        grid_spec=pltpu.PrefetchScalarGridSpec(
            num_scalar_prefetch=1,
            grid=(micro,),
            in_specs=[
                pl.BlockSpec((1, rows, width), lambda k, order: (order[k], 0, 0)),
                pl.BlockSpec((RANK, width), lambda k, order: (0, 0)),
            ],
            out_specs=pl.BlockSpec((rows, RANK), lambda k, order: (k, 0)),
        ),
        out_shape=jax.ShapeDtypeStruct((ROWS, RANK), BF),
        compiler_params=pltpu.CompilerParams(vmem_limit_bytes=VMEM),
        cost_estimate=cost(8),
    )(order, cotangent, up)


def cross_kernel(xs, up, down, squares, pay):
    def ups(base, n):
        return up[base : base + n].reshape(n * RANK, F)

    for s in range(N):
        own = xs[N - 1 - s]
        base, t = BLK * (s // BLK), s % BLK
        pay[:, cols((A1 if base else A2) + t)] = dot(own, down[s], NN).astype(BF)
        if t:
            at = (X1 if base else X2) + PAIR_AT[t, 0]
            pay[:, cols(at, t)] = dot(own, ups(base, t), NT).astype(BF)
    pay[:, cols(SQ)] = squares[...]


def rank_kernel(first, tops, sums, power, weights, coef):
    base = BLK if first else 0

    def total(ref, m, n=1):
        return jnp.sum(ref[:, cols(m, n)].astype(F32).reshape(N, ROWN, n * RANK), axis=0)

    power = total(power, 0)

    def activation(s):
        mean = (power[:, s : s + 1] + power[:, N + s : N + s + 1]) * (1.0 / WIDTH)
        scale = lax.rsqrt(mean + 1e-05)
        act = total(sums, A1 + s % BLK) * scale
        return scale, act, jax.nn.sigmoid(act)

    if first:
        grads = [tops[ROWN * (BLK + t) : ROWN * (BLK + t + 1), :] for t in range(BLK)]
    else:
        grads = [total(tops, t) for t in range(BLK)]
    lane = lax.broadcasted_iota(jnp.int32, (ROWN, RANK), 1)
    shares = jnp.zeros((ROWN, RANK), F32)
    for j in range(BLK - 1, -1, -1):
        scale, act, sig = activation(base + j)
        d_act = grads[j] * sig * (1.0 + act * (1.0 - sig))
        inner = jnp.sum(d_act * act, axis=1, keepdims=True) * (1.0 / WIDTH)
        sent = (d_act * scale).astype(BF)
        share = (inner * scale * scale).astype(BF).astype(F32)
        coef[:, cols(j)] = jnp.tile(d_act * scale, (N, 1)).astype(BF)
        coef[:, cols(BLK + 1 + j)] = jnp.tile(act * sig, (N, 1)).astype(BF)
        shares = jnp.where(lane == j, share, shares)
        if j:
            mats = []
            for i in range(j):
                gap = j - i
                held, d = (i, gap) if gap <= HALF else (j, BLK - gap)
                mats.append(weights[held, cols(d - 1), :])
            step = dot(sent, jnp.concatenate(mats, axis=1), NN)
            step = step - share * total(sums, X1 + PAIR_AT[j, 0], j)
            for i in range(j):
                grads[i] = grads[i] + step[:, cols(i)]
    coef[:, cols(BLK)] = jnp.tile(shares, (N, 1)).astype(BF)


def update_kernel(first, core, top, coef, xs, down, *refs):
    if first:
        up, out, pay, carry, parts = refs
    else:
        _, out, kept, sent = refs
    grad = top[...].astype(F32)
    shares = coef[:, cols(BLK)].astype(F32)
    for j in range(BLK - 1, -1, -1):
        low = dot(coef[:, cols(j)], down[j], NT)
        grad = grad + low - shares[:, j : j + 1] * xs[BLK - 1 - j].astype(F32)
        out[j] = grad.astype(BF)
    if first:
        carry[...] = grad
        pay[...] = dot(grad.astype(BF), up[...].reshape(BLK * RANK, F), NT).astype(BF)
    own = jnp.full((64, RANK), core[0], jnp.int32) == 0
    for j in range(BLK):
        upstream = out[j + 1] if j < BLK - 1 else top[...].astype(BF)
        down_part = dot(xs[BLK - 1 - j], coef[:, cols(j)], TN)
        up_part = dot(upstream, coef[:, cols(BLK + 1 + j)], TN)
        for n in range(N // 2):
            at = 64 * n
            even = jnp.concatenate([down_part[at : at + 32], up_part[at : at + 32]], axis=0)
            odd = jnp.concatenate(
                [down_part[at + 32 : at + 64], up_part[at + 32 : at + 64]], axis=0
            )
            if first:
                parts[2 * n, j] = even.astype(BF)
                parts[2 * n + 1, j] = odd.astype(BF)
            else:
                kept[n, j] = jnp.where(own, even, odd).astype(BF)
                sent[n, j] = jnp.where(own, odd, even).astype(BF)


def pair_kernel(kept, other, out):
    out[...] = (kept[...].astype(F32) + other[...].astype(F32)).astype(BF)


def replica_parts(kept, sent):
    other = lax.ppermute(sent, "dp", [(p, p ^ 1) for p in range(N)])
    (pairs,) = call(pair_kernel, [(kept.shape, BF)], us=2)(kept, other)
    groups = [list(range(n, N, 2)) for n in range(2)]
    return lax.all_to_all(pairs, "dp", 0, 0, axis_index_groups=groups)


def sum_kernel(first, parts, _, out):
    for t in range(BLK):
        total = parts[0, t].astype(F32)
        for n in range(1, N // 2):
            total = total + parts[n, t].astype(F32)
        total = total.astype(BF)
        for n in range(4):
            out[t, :, cols(n)] = total[16 * n : 16 * n + 16]
            out[BLK + t, :, cols(n)] = first[t, 16 * n : 16 * n + 16, :]


def finish_kernel(rep, src, sums, gain, out, down, up):
    for c in range(4):
        for a in range(4):
            tiles = turned([src[4 * c + m, :, cols(a)] for m in range(4)])
            for b, tile in enumerate(tiles):
                at = F * (4 * a + b) + RANK * c
                out[0, :, at : at + RANK] = tile

    @pl.when(pl.program_id(0) == 0)
    def _():
        row = lax.broadcasted_iota(jnp.int32, (32, F), 0)
        lane = lax.broadcasted_iota(jnp.int32, (32, F), 1)
        for m in range(4):
            ups = []
            for f in range(4 * m, 4 * m + 4):
                hit = jnp.where(lane == row + 32 * f, gain[...], 0.0)
                column = jnp.sum(hit, axis=1, keepdims=True)
                tiles = [sums[f, :, cols(n)].astype(F32) for n in range(4)]
                down[32 * f : 32 * f + 32, :] = jnp.concatenate(tiles[:2], axis=0) * column
                ups += tiles[2:]
            up[:, cols(m)] = jnp.concatenate(ups, axis=0).T


def finished(received, rep, gain, micro):
    rows = ROWS // micro
    return pl.pallas_call(
        finish_kernel,
        grid_spec=pltpu.PrefetchScalarGridSpec(
            num_scalar_prefetch=1,
            grid=(micro,),
            in_specs=[
                pl.BlockSpec((N, rows, F), lambda k, rep: (0, k, 0)),
                pl.BlockSpec((N, 16, F), lambda k, rep: (0, ROWS // 16, 0)),
                pl.BlockSpec((1, F), lambda k, rep: (0, rep[0])),
            ],
            out_specs=[
                pl.BlockSpec((1, rows, WIDTH), lambda k, rep: (k, 0, 0)),
                pl.BlockSpec((F, RANK), lambda k, rep: (0, 0)),
                pl.BlockSpec((RANK, F), lambda k, rep: (0, 0)),
            ],
        ),
        out_shape=[
            jax.ShapeDtypeStruct((micro, rows, WIDTH), BF),
            jax.ShapeDtypeStruct((F, RANK), F32),
            jax.ShapeDtypeStruct((RANK, F), F32),
        ],
        compiler_params=pltpu.CompilerParams(vmem_limit_bytes=VMEM),
        cost_estimate=cost(5),
    )(rep.reshape(1), received, received, gain)


def tie_kernel(*refs):
    pass


def tie(block, *others):
    anywhere = pl.BlockSpec(memory_space=pl.ANY)
    return call(
        tie_kernel,
        [(block.shape, block.dtype)],
        us=1,
        in_specs=[anywhere] * (1 + len(others)),
        out_specs=[anywhere],
        input_output_aliases={0: 0},
    )(block, *others)[0]


def after(block, *others):
    return lax.optimization_barrier((block, *others))[0]


def whole(shape):
    return pl.BlockSpec(shape, lambda n: (0,) * len(shape))


def half(shape, at):
    return pl.BlockSpec(shape, lambda n: (at,) + (0,) * (len(shape) - 1))


def swap(block):
    return lax.all_to_all(block, "section", 0, 0, tiled=True)


def body(parked, cotangent, park_table, run_order, norm_gain, down_weight, up_weight):
    me = lax.axis_index("section")
    rep = lax.axis_index("dp")
    micro, rows, width = cotangent.shape

    thin = thin_weights(rep, down_weight[0], up_weight[0], norm_gain)
    thin = lax.all_to_all(thin, "section", 0, 0)

    slot_row = lax.dynamic_index_in_dim(park_table, me, 0, keepdims=False)
    hit = (run_order[:, None] == slot_row[None, :]).astype(jnp.int32)
    slots = jnp.sum(hit * jnp.arange(micro, dtype=jnp.int32)[None, :], axis=1)
    pieces = split_rows(parked[0], slots)
    big = lax.all_gather(tie(thin, pieces), "dp")
    xs = lax.all_to_all(after(pieces, thin), "section", 0, 0)
    cot = lax.dynamic_index_in_dim(split_rows(cotangent, run_order), me, 0, keepdims=False)

    side, near = BLK * (rep // BLK), rep % BLK
    far = (near + jnp.arange(1, HALF + 1, dtype=jnp.int32)) % BLK
    smem = pl.BlockSpec(memory_space=pltpu.SMEM)
    (w_part,) = call(
        product_kernel,
        [((HALF * RANK, RANK), BF)],
        in_specs=[smem, smem, pl.BlockSpec(memory_space=pltpu.VMEM)],
    )(side + jnp.maximum(near, far), side + jnp.minimum(near, far), big)
    ups, downs, squares = call(
        layout_kernel, [((N, RANK, F), BF), ((N, F, RANK), BF), ((ROWS, RANK), BF)]
    )(big, xs)
    tops = top_products(cotangent, run_order, up_weight[0]).reshape(N, ROWN, RANK)
    mixed = jnp.concatenate([w_part.reshape(N, -1, RANK), tops], axis=1)
    mixed = lax.all_to_all(after(mixed, xs), "section", 0, 0).astype(F32)
    w_sum = mixed[:, :-ROWN].sum(0).astype(BF)
    tops = mixed[:, -ROWN:].reshape(N * ROWN, RANK)
    w_all = jnp.broadcast_to(w_sum[None], (N,) + w_sum.shape).reshape(-1, RANK)
    w_all = swap(tie(w_all, ups))

    (pay1,) = call(cross_kernel, [((ROWS, MATS * RANK), BF)])(xs, ups, downs, squares)
    got1 = swap(after(pay1, w_all))
    w_all = lax.all_gather(w_all, "dp").reshape(N, HALF * RANK, RANK)
    coef_out = ((ROWS, (2 * BLK + 1) * RANK), BF)

    def rank_steps(block, tops):
        return call(
            functools.partial(rank_kernel, block == 1),
            [coef_out],
            grid=(1,),
            in_specs=[
                whole(tops.shape),
                pl.BlockSpec((ROWS, SIDE * RANK), lambda n: (0, 1 - block)),
                pl.BlockSpec((ROWS, RANK), lambda n: (0, SQ)),
                half((BLK,) + w_all.shape[1:], block),
            ],
            out_specs=[whole(coef_out[0])],
        )(tops, got1, got1, w_all)[0]

    coef1 = rank_steps(1, tops)
    coef1 = swap(coef1)

    half_rows, half_down, half_up = (BLK, ROWS, F), (BLK, F, RANK), (BLK, RANK, F)
    core = (rep % 2).reshape(1)
    smem = pl.BlockSpec(memory_space=pltpu.SMEM)
    halves = (N // 2, BLK, 64, RANK)
    grads1, pay3, carry, parts1 = call(
        functools.partial(update_kernel, True),
        [
            ((N, SENT, F), BF),
            ((ROWS, BLK * RANK), BF),
            ((ROWS, F), F32),
            ((N, BLK, 64, RANK), BF),
        ],
        grid=(1,),
        in_specs=[
            smem,
            whole((ROWS, F)),
            whole(coef1.shape),
            half(half_rows, 0),
            half(half_down, 1),
            half(half_up, 0),
        ],
        out_specs=[
            half(half_rows, 1),
            whole((ROWS, BLK * RANK)),
            whole((ROWS, F)),
            whole((N, BLK, 64, RANK)),
        ],
    )(core, cot, coef1, xs, downs, ups)
    got3 = swap(pay3)

    def reduced(parts):
        return lax.psum_scatter(parts, "dp", scatter_dimension=0, tiled=True)[0]

    total1 = reduced(parts1)

    coef2 = rank_steps(0, got3)
    coef2 = swap(coef2)
    grads2, kept, sent = call(
        functools.partial(update_kernel, False),
        [((N, SENT, F), BF), (halves, BF), (halves, BF)],
        grid=(1,),
        in_specs=[
            smem,
            whole((ROWS, F)),
            whole(coef2.shape),
            half(half_rows, 1),
            half(half_down, 0),
            pl.BlockSpec(memory_space=pl.ANY),
        ],
        out_specs=[half(half_rows, 0), whole(halves), whole(halves)],
        input_output_aliases={5: 0},
    )(core, carry, coef2, xs, downs, grads1)
    parts2 = replica_parts(kept, sent)
    (sent,) = call(
        sum_kernel,
        [((N, SENT, F), BF)],
        grid=(1,),
        in_specs=[
            whole(total1.shape),
            whole(parts2.shape),
            pl.BlockSpec(memory_space=pl.ANY),
        ],
        out_specs=[pl.BlockSpec((N, 16, F), lambda n: (0, ROWS // 16, 0))],
        input_output_aliases={2: 0},
    )(total1, parts2, grads2)
    received = lax.all_to_all(sent, "section", 0, 0)
    out, down_grad, up_grad = finished(received, rep, norm_gain, micro)
    return (out[None], down_grad[None], up_grad[None])


def solution(mesh):
    placed = (
        P("section", None, "dp", None),
        P(None, "dp", None),
        P(),
        P(),
        P("section", None),
        P("section", None, None),
        P("section", None, None),
    )
    return jax.shard_map(
        body,
        mesh=mesh,
        in_specs=placed,
        out_specs=(
            P("section", None, "dp", None),
            P("section", "dp", None),
            P("section", None, "dp"),
        ),
        check_vma=False,
    )
```

```python
import functools
import jax
import jax.numpy as jnp
from jax import lax
from jax.experimental import pallas as pl
from jax.experimental.pallas import tpu as pltpu
from jax.sharding import PartitionSpec as P

N = 16
BLK = 8
ROWS = 128
ROWN = ROWS // N
F = 512
RANK = 128
WIDTH = N * F
PAIRS = [(j, i) for j in range(BLK - 1, 0, -1) for i in range(j)]
PAIR_AT = {pair: n for n, pair in enumerate(PAIRS)}
NP = len(PAIRS)
VMEM = 46 << 20
SIDE = NP + BLK
X1, A1 = 0, NP
X2, A2 = SIDE, SIDE + NP
SQ = 2 * SIDE
MATS = SQ + 1
BF = jnp.bfloat16
F32 = jnp.float32

HALF = BLK // 2
SENT = ROWS + 16

NT = (((1,), (1,)), ((), ()))
NN = (((1,), (0,)), ((), ()))
TN = (((0,), (0,)), ((), ()))


def dot(a, b, dims):
    return lax.dot_general(a, b, dims, preferred_element_type=F32)


def cols(m, n=1):
    return slice(m * RANK, (m + n) * RANK)


def cost(us):
    return pl.CostEstimate(flops=0, bytes_accessed=int(us * 3e6), transcendentals=0)


def call(kernel, outs, us=4, **kw):
    return pl.pallas_call(
        kernel,
        out_shape=[jax.ShapeDtypeStruct(s, d) for s, d in outs],
        compiler_params=pltpu.CompilerParams(vmem_limit_bytes=VMEM),
        cost_estimate=cost(us),
        **kw,
    )


def turned(tiles):
    quarter = lax.broadcasted_iota(jnp.int32, tiles[0].shape, 1) // 32
    for bit in range(2):
        step = 1 << bit
        low = (quarter >> bit) % 2 == 0
        tiles = [
            jnp.where(low, tiles[b], pltpu.roll(tiles[b + step], 32 * step, 1))
            if (b >> bit) % 2 == 0
            else jnp.where(low, pltpu.roll(tiles[b - step], RANK - 32 * step, 1), tiles[b])
            for b in range(4)
        ]
    return tiles


def split_kernel(slots, src, dst):
    for c in range(4):
        for a in range(4):
            tiles = [
                src[0, :, F * (4 * a + b) + RANK * c : F * (4 * a + b) + RANK * (c + 1)]
                for b in range(4)
            ]
            for m, tile in enumerate(turned(tiles)):
                dst[4 * c + m, 0, :, cols(a)] = tile


def split_rows(parked, slots):
    micro, rows, width = parked.shape
    return pl.pallas_call(
        split_kernel,
        grid_spec=pltpu.PrefetchScalarGridSpec(
            num_scalar_prefetch=1,
            grid=(micro,),
            in_specs=[pl.BlockSpec((1, rows, width), lambda k, slots: (slots[k], 0, 0))],
            out_specs=pl.BlockSpec((N, 1, rows, F), lambda k, slots: (0, k, 0, 0)),
        ),
        out_shape=jax.ShapeDtypeStruct((N, micro, rows, F), BF),
        compiler_params=pltpu.CompilerParams(vmem_limit_bytes=VMEM),
        cost_estimate=cost(4),
    )(slots, parked).reshape(N, micro * rows, F)


def thin_kernel(rep, down, up, gain, out):
    row = lax.broadcasted_iota(jnp.int32, (32, F), 0)
    lane = lax.broadcasted_iota(jnp.int32, (32, F), 1)
    for c in range(4):
        for a in range(2):
            at = [F * (4 * a + b) + RANK * c for b in range(4)]
            tiles = turned([up[:, n : n + RANK] for n in at])
            for m, tile in enumerate(tiles):
                out[4 * c + m, 16 * a : 16 * a + 16, :] = tile
    for f in range(N):
        column = jnp.sum(jnp.where(lane == row + 32 * f, gain[...], 0.0), axis=1, keepdims=True)
        out[f, 32:64, :] = (down[0, f].astype(F32) * column).astype(BF)


def thin_weights(rep, down, up, gain):
    return pl.pallas_call(
        thin_kernel,
        grid_spec=pltpu.PrefetchScalarGridSpec(
            num_scalar_prefetch=1,
            grid=(1,),
            in_specs=[
                pl.BlockSpec((1, N, 32, RANK), lambda n, rep: (rep[0], 0, 0, 0)),
                pl.BlockSpec((16, WIDTH // 2), lambda n, rep: (rep[0] // 2, rep[0] % 2)),
                pl.BlockSpec((1, F), lambda n, rep: (0, rep[0])),
            ],
            out_specs=pl.BlockSpec((N, 64, RANK), lambda n, rep: (0, 0, 0)),
        ),
        out_shape=jax.ShapeDtypeStruct((N, 64, RANK), BF),
        compiler_params=pltpu.CompilerParams(vmem_limit_bytes=VMEM),
        cost_estimate=cost(2),
    )(rep.reshape(1), down.reshape(N, N, 32, RANK), up, gain)


def weight_kernel(big, up, down):
    for s in range(N):
        for p in range(N):
            r, h = p // 2, p % 2
            for c in range(2):
                at = (2 * h + c) * RANK
                up[s, 16 * r : 16 * r + 16, at : at + RANK] = big[p, s, 16 * c : 16 * c + 16, :]
            down[s, 32 * p : 32 * p + 32, :] = big[p, s, 32:64, :]


def product_kernel(jx, ix, big, out):
    for d in range(HALF):
        tiles = [big[p, ix[d], 16 * c : 16 * c + 16, :] for p in range(N) for c in range(2)]
        rows = [jnp.concatenate(tiles[4 * r : 4 * r + 4], axis=1) for r in range(N // 2)]
        up = jnp.concatenate(rows, axis=0)
        down = jnp.concatenate([big[p, jx[d], 32:64, :] for p in range(N)], axis=0)
        out[cols(d), :] = dot(down.T, up, NT).astype(BF)


def top_kernel(order, cot, up, out):
    out[...] = dot(cot[0], up[...], NT).astype(BF)


def top_products(cotangent, order, up):
    micro, rows, width = cotangent.shape
    return pl.pallas_call(
        top_kernel,
        grid_spec=pltpu.PrefetchScalarGridSpec(
            num_scalar_prefetch=1,
            grid=(micro,),
            in_specs=[
                pl.BlockSpec((1, rows, width), lambda k, order: (order[k], 0, 0)),
                pl.BlockSpec((RANK, width), lambda k, order: (0, 0)),
            ],
            out_specs=pl.BlockSpec((rows, RANK), lambda k, order: (k, 0)),
        ),
        out_shape=jax.ShapeDtypeStruct((ROWS, RANK), BF),
        compiler_params=pltpu.CompilerParams(vmem_limit_bytes=VMEM),
        cost_estimate=cost(8),
    )(order, cotangent, up)


def cross_kernel(xs, up, down, pay):
    def ups(base, n):
        return up[base : base + n].reshape(n * RANK, F)

    lane = lax.broadcasted_iota(jnp.int32, (ROWS, RANK), 1)
    total = jnp.zeros((ROWS, RANK), F32)
    for s in range(N):
        own = xs[N - 1 - s]
        base, t = BLK * (s // BLK), s % BLK
        pay[:, cols((A1 if base else A2) + t)] = dot(own, down[s], NN).astype(BF)
        if t:
            at = (X1 if base else X2) + PAIR_AT[t, 0]
            pay[:, cols(at, t)] = dot(own, ups(base, t), NT).astype(BF)
        wide = own.astype(F32)
        power = jnp.sum(wide * wide, axis=1, keepdims=True)
        high = power.astype(BF).astype(F32)
        total = jnp.where(lane == s, high, total)
        total = jnp.where(lane == N + s, power - high, total)
    pay[:, cols(SQ)] = total.astype(BF)


def rank_kernel(first, tops, sums, power, weights, coef):
    base = BLK if first else 0

    def total(ref, m, n=1):
        return jnp.sum(ref[:, cols(m, n)].astype(F32).reshape(N, ROWN, n * RANK), axis=0)

    power = total(power, 0)

    def activation(s):
        mean = (power[:, s : s + 1] + power[:, N + s : N + s + 1]) * (1.0 / WIDTH)
        scale = lax.rsqrt(mean + 1e-05)
        act = total(sums, A1 + s % BLK) * scale
        return scale, act, jax.nn.sigmoid(act)

    if first:
        grads = [tops[ROWN * (BLK + t) : ROWN * (BLK + t + 1), :] for t in range(BLK)]
    else:
        grads = [total(tops, t) for t in range(BLK)]
    lane = lax.broadcasted_iota(jnp.int32, (ROWN, RANK), 1)
    shares = jnp.zeros((ROWN, RANK), F32)
    for j in range(BLK - 1, -1, -1):
        scale, act, sig = activation(base + j)
        d_act = grads[j] * sig * (1.0 + act * (1.0 - sig))
        inner = jnp.sum(d_act * act, axis=1, keepdims=True) * (1.0 / WIDTH)
        sent = (d_act * scale).astype(BF)
        share = (inner * scale * scale).astype(BF).astype(F32)
        coef[:, cols(j)] = jnp.tile(d_act * scale, (N, 1)).astype(BF)
        coef[:, cols(BLK + 1 + j)] = jnp.tile(act * sig, (N, 1)).astype(BF)
        shares = jnp.where(lane == j, share, shares)
        if j:
            mats = []
            for i in range(j):
                gap = j - i
                held, d = (i, gap) if gap <= HALF else (j, BLK - gap)
                mats.append(weights[held, cols(d - 1), :])
            step = dot(sent, jnp.concatenate(mats, axis=1), NN)
            step = step - share * total(sums, X1 + PAIR_AT[j, 0], j)
            for i in range(j):
                grads[i] = grads[i] + step[:, cols(i)]
    coef[:, cols(BLK)] = jnp.tile(shares, (N, 1)).astype(BF)


def update_kernel(first, core, top, coef, xs, down, *refs):
    if first:
        up, out, pay, carry, parts = refs
    else:
        _, out, kept, sent = refs
    grad = top[...].astype(F32)
    shares = coef[:, cols(BLK)].astype(F32)
    for j in range(BLK - 1, -1, -1):
        low = dot(coef[:, cols(j)], down[j], NT)
        grad = grad + low - shares[:, j : j + 1] * xs[BLK - 1 - j].astype(F32)
        out[j] = grad.astype(BF)
    if first:
        carry[...] = grad
        pay[...] = dot(grad.astype(BF), up[...].reshape(BLK * RANK, F), NT).astype(BF)
    own = jnp.full((64, RANK), core[0], jnp.int32) == 0
    for j in range(BLK):
        upstream = out[j + 1] if j < BLK - 1 else top[...].astype(BF)
        down_part = dot(xs[BLK - 1 - j], coef[:, cols(j)], TN)
        up_part = dot(upstream, coef[:, cols(BLK + 1 + j)], TN)
        for n in range(N // 2):
            at = 64 * n
            even = jnp.concatenate([down_part[at : at + 32], up_part[at : at + 32]], axis=0)
            odd = jnp.concatenate(
                [down_part[at + 32 : at + 64], up_part[at + 32 : at + 64]], axis=0
            )
            if first:
                parts[2 * n, j] = even.astype(BF)
                parts[2 * n + 1, j] = odd.astype(BF)
            else:
                kept[n, j] = jnp.where(own, even, odd).astype(BF)
                sent[n, j] = jnp.where(own, odd, even).astype(BF)


def pair_kernel(kept, other, out):
    out[...] = (kept[...].astype(F32) + other[...].astype(F32)).astype(BF)


def replica_parts(kept, sent):
    other = lax.ppermute(sent, "dp", [(p, p ^ 1) for p in range(N)])
    (pairs,) = call(pair_kernel, [(kept.shape, BF)], us=2)(kept, other)
    groups = [list(range(n, N, 2)) for n in range(2)]
    return lax.all_to_all(pairs, "dp", 0, 0, axis_index_groups=groups)


def sum_kernel(first, parts, _, out):
    for t in range(BLK):
        total = parts[0, t].astype(F32)
        for n in range(1, N // 2):
            total = total + parts[n, t].astype(F32)
        total = total.astype(BF)
        for n in range(4):
            out[t, :, cols(n)] = total[16 * n : 16 * n + 16]
            out[BLK + t, :, cols(n)] = first[t, 16 * n : 16 * n + 16, :]


def finish_kernel(rep, src, sums, gain, out, down, up):
    for c in range(4):
        for a in range(4):
            tiles = turned([src[4 * c + m, :, cols(a)] for m in range(4)])
            for b, tile in enumerate(tiles):
                at = F * (4 * a + b) + RANK * c
                out[0, :, at : at + RANK] = tile

    @pl.when(pl.program_id(0) == 0)
    def _():
        row = lax.broadcasted_iota(jnp.int32, (32, F), 0)
        lane = lax.broadcasted_iota(jnp.int32, (32, F), 1)
        for m in range(4):
            ups = []
            for f in range(4 * m, 4 * m + 4):
                hit = jnp.where(lane == row + 32 * f, gain[...], 0.0)
                column = jnp.sum(hit, axis=1, keepdims=True)
                tiles = [sums[f, :, cols(n)].astype(F32) for n in range(4)]
                down[32 * f : 32 * f + 32, :] = jnp.concatenate(tiles[:2], axis=0) * column
                ups += tiles[2:]
            up[:, cols(m)] = jnp.concatenate(ups, axis=0).T


def finished(received, rep, gain, micro):
    rows = ROWS // micro
    return pl.pallas_call(
        finish_kernel,
        grid_spec=pltpu.PrefetchScalarGridSpec(
            num_scalar_prefetch=1,
            grid=(micro,),
            in_specs=[
                pl.BlockSpec((N, rows, F), lambda k, rep: (0, k, 0)),
                pl.BlockSpec((N, 16, F), lambda k, rep: (0, ROWS // 16, 0)),
                pl.BlockSpec((1, F), lambda k, rep: (0, rep[0])),
            ],
            out_specs=[
                pl.BlockSpec((1, rows, WIDTH), lambda k, rep: (k, 0, 0)),
                pl.BlockSpec((F, RANK), lambda k, rep: (0, 0)),
                pl.BlockSpec((RANK, F), lambda k, rep: (0, 0)),
            ],
        ),
        out_shape=[
            jax.ShapeDtypeStruct((micro, rows, WIDTH), BF),
            jax.ShapeDtypeStruct((F, RANK), F32),
            jax.ShapeDtypeStruct((RANK, F), F32),
        ],
        compiler_params=pltpu.CompilerParams(vmem_limit_bytes=VMEM),
        cost_estimate=cost(5),
    )(rep.reshape(1), received, received, gain)


def tie_kernel(*refs):
    pass


def tie(block, *others):
    anywhere = pl.BlockSpec(memory_space=pl.ANY)
    return call(
        tie_kernel,
        [(block.shape, block.dtype)],
        us=1,
        in_specs=[anywhere] * (1 + len(others)),
        out_specs=[anywhere],
        input_output_aliases={0: 0},
    )(block, *others)[0]


def after(block, *others):
    return lax.optimization_barrier((block, *others))[0]


def whole(shape):
    return pl.BlockSpec(shape, lambda n: (0,) * len(shape))


def half(shape, at):
    return pl.BlockSpec(shape, lambda n: (at,) + (0,) * (len(shape) - 1))


def swap(block):
    return lax.all_to_all(block, "section", 0, 0, tiled=True)


def body(parked, cotangent, park_table, run_order, norm_gain, down_weight, up_weight):
    me = lax.axis_index("section")
    rep = lax.axis_index("dp")
    micro, rows, width = cotangent.shape

    thin = thin_weights(rep, down_weight[0], up_weight[0], norm_gain)
    thin = lax.all_to_all(thin, "section", 0, 0)

    slot_row = lax.dynamic_index_in_dim(park_table, me, 0, keepdims=False)
    hit = (run_order[:, None] == slot_row[None, :]).astype(jnp.int32)
    slots = jnp.sum(hit * jnp.arange(micro, dtype=jnp.int32)[None, :], axis=1)
    pieces = split_rows(parked[0], slots)
    big = lax.all_gather(tie(thin, pieces), "dp")
    xs = lax.all_to_all(after(pieces, thin), "section", 0, 0)
    cot = lax.dynamic_index_in_dim(split_rows(cotangent, run_order), me, 0, keepdims=False)

    side, near = BLK * (rep // BLK), rep % BLK
    far = (near + jnp.arange(1, HALF + 1, dtype=jnp.int32)) % BLK
    smem = pl.BlockSpec(memory_space=pltpu.SMEM)
    (w_part,) = call(
        product_kernel,
        [((HALF * RANK, RANK), BF)],
        in_specs=[smem, smem, pl.BlockSpec(memory_space=pltpu.VMEM)],
    )(side + jnp.maximum(near, far), side + jnp.minimum(near, far), big)
    ups, downs = call(weight_kernel, [((N, RANK, F), BF), ((N, F, RANK), BF)])(big)
    tops = top_products(cotangent, run_order, up_weight[0]).reshape(N, ROWN, RANK)
    mixed = jnp.concatenate([w_part.reshape(N, -1, RANK), tops], axis=1)
    mixed = lax.all_to_all(after(mixed, xs), "section", 0, 0).astype(F32)
    w_sum = mixed[:, :-ROWN].sum(0).astype(BF)
    tops = mixed[:, -ROWN:].reshape(N * ROWN, RANK)
    w_all = jnp.broadcast_to(w_sum[None], (N,) + w_sum.shape).reshape(-1, RANK)
    w_all = swap(tie(w_all, ups))

    (pay1,) = call(cross_kernel, [((ROWS, MATS * RANK), BF)])(xs, ups, downs)
    got1 = swap(after(pay1, w_all))
    w_all = lax.all_gather(w_all, "dp").reshape(N, HALF * RANK, RANK)
    coef_out = ((ROWS, (2 * BLK + 1) * RANK), BF)

    def rank_steps(block, tops):
        return call(
            functools.partial(rank_kernel, block == 1),
            [coef_out],
            grid=(1,),
            in_specs=[
                whole(tops.shape),
                pl.BlockSpec((ROWS, SIDE * RANK), lambda n: (0, 1 - block)),
                pl.BlockSpec((ROWS, RANK), lambda n: (0, SQ)),
                half((BLK,) + w_all.shape[1:], block),
            ],
            out_specs=[whole(coef_out[0])],
        )(tops, got1, got1, w_all)[0]

    coef1 = rank_steps(1, tops)
    coef1 = swap(coef1)

    half_rows, half_down, half_up = (BLK, ROWS, F), (BLK, F, RANK), (BLK, RANK, F)
    core = (rep % 2).reshape(1)
    smem = pl.BlockSpec(memory_space=pltpu.SMEM)
    halves = (N // 2, BLK, 64, RANK)
    grads1, pay3, carry, parts1 = call(
        functools.partial(update_kernel, True),
        [
            ((N, SENT, F), BF),
            ((ROWS, BLK * RANK), BF),
            ((ROWS, F), F32),
            ((N, BLK, 64, RANK), BF),
        ],
        grid=(1,),
        in_specs=[
            smem,
            whole((ROWS, F)),
            whole(coef1.shape),
            half(half_rows, 0),
            half(half_down, 1),
            half(half_up, 0),
        ],
        out_specs=[
            half(half_rows, 1),
            whole((ROWS, BLK * RANK)),
            whole((ROWS, F)),
            whole((N, BLK, 64, RANK)),
        ],
    )(core, cot, coef1, xs, downs, ups)
    got3 = swap(pay3)

    def reduced(parts):
        return lax.psum_scatter(parts, "dp", scatter_dimension=0, tiled=True)[0]

    total1 = reduced(parts1)

    coef2 = rank_steps(0, got3)
    coef2 = swap(coef2)
    grads2, kept, sent = call(
        functools.partial(update_kernel, False),
        [((N, SENT, F), BF), (halves, BF), (halves, BF)],
        grid=(1,),
        in_specs=[
            smem,
            whole((ROWS, F)),
            whole(coef2.shape),
            half(half_rows, 1),
            half(half_down, 0),
            pl.BlockSpec(memory_space=pl.ANY),
        ],
        out_specs=[half(half_rows, 0), whole(halves), whole(halves)],
        input_output_aliases={5: 0},
    )(core, carry, coef2, xs, downs, grads1)
    parts2 = replica_parts(kept, sent)
    (sent,) = call(
        sum_kernel,
        [((N, SENT, F), BF)],
        grid=(1,),
        in_specs=[
            whole(total1.shape),
            whole(parts2.shape),
            pl.BlockSpec(memory_space=pl.ANY),
        ],
        out_specs=[pl.BlockSpec((N, 16, F), lambda n: (0, ROWS // 16, 0))],
        input_output_aliases={2: 0},
    )(total1, parts2, grads2)
    received = lax.all_to_all(sent, "section", 0, 0)
    out, down_grad, up_grad = finished(received, rep, norm_gain, micro)
    return (out[None], down_grad[None], up_grad[None])


def solution(mesh):
    placed = (
        P("section", None, "dp", None),
        P(None, "dp", None),
        P(),
        P(),
        P("section", None),
        P("section", None, None),
        P("section", None, None),
    )
    return jax.shard_map(
        body,
        mesh=mesh,
        in_specs=placed,
        out_specs=(
            P("section", None, "dp", None),
            P("section", "dp", None),
            P("section", None, "dp"),
        ),
        check_vma=False,
    )
```
